256 devices in a mesh: blk: 64 (over z, x, y_hi), rep: 4 (over y_lo, core).
Axes of the slice: x: 4, y: 4 (y_hi: 2, y_lo: 2; y = y_hi * 2 + y_lo), z: 8, core: 2. Of those that a mesh axis runs over, the one named last changes fastest.
Arguments:
- node_input: bfloat16 [65536, 1024], P(('blk', 'rep')), may hold values from -6 to 6
- output_grad: bfloat16 [65536, 1024], P(('blk', 'rep')), may hold values from -6 to 6
- saved_output: bfloat16 [65536, 1024], P(('blk', 'rep')), may hold values from -3 to 3
- weight_query: bfloat16 [1024, 1024], replicated, may hold values from -0.1875 to 0.1875
- weight_key: bfloat16 [1024, 1024], replicated, may hold values from -0.1875 to 0.1875
- weight_value: bfloat16 [1024, 1024], replicated, may hold values from -0.1875 to 0.1875
- weight_out: bfloat16 [1024, 1024], replicated, may hold values from -0.1875 to 0.1875
- tile_slots: int32 [256, 2, 12], P(('blk', 'rep')), may hold values from 0 to 9, as said below
- tile_mask: int32 [256, 12, 128, 128], P(('blk', 'rep')), may hold values from 0 to 1
- tile_count: int32 [256], P(('blk', 'rep')), may hold values from 3 to 12, as said below
Outputs:
- input_grad: bfloat16 [65536, 1024], P(('blk', 'rep'))
- query_weight_grad: bfloat16 [64, 1024, 1024], P('blk', 'rep')
- key_weight_grad: bfloat16 [64, 1024, 1024], P('blk', 'rep')
- value_weight_grad: bfloat16 [64, 1024, 1024], P('blk', 'rep')
- out_weight_grad: bfloat16 [64, 1024, 1024], P('blk', 'rep')
The draws below stay inside these ranges and needn't reach their ends.
Inputs may be any that keep to these rules, and one draw needn't show every extreme that they name: `tile_slots`: within one group no two slots name the same pair of row tile and column tile; row tiles lie below 8, column tiles below (5) * 2, in every slot. `tile_count`: some group has all 12 slots live in every draw.
All inputs are finite; a program needn't handle non-finite values.
Results may differ from the reference program's by a relative error of at most 0.02.
Values may be sent and summed in bfloat16 or wider, within the bound.
No kernel may reach another device: no remote copies, remote signals or barrier semaphores. Data moves between devices by JAX's collectives and lax.ppermute only.
A program may use at most 128 MiB of HBM per device.

```python
import jax
import jax.numpy as jnp
from jax import lax

HEADS = 16
HEAD_DIM = 64
D = 1024
TS = 128
REACH = 2
R_DEV = 256
TILE_DEV = 12
NODES = 65536
N_BLK = 64
N_REP = 4


def draw_tile_slots(key, part):
    key = jax.random.fold_in(key, 11)
    row_tiles = N_REP * R_DEV // TS
    col_tiles = (2 * REACH + 1) * R_DEV // TS
    device_keys = jax.random.split(key, N_BLK * N_REP)

    def one_device(device_key):
        picked = jax.random.permutation(device_key, row_tiles * col_tiles)[:TILE_DEV]
        return jnp.stack([picked // col_tiles, picked % col_tiles]).astype(jnp.int32)
    return jax.vmap(one_device)(device_keys)


def draw_tile_mask(key, part):
    key = jax.random.fold_in(key, 12)
    level_key, entry_key = jax.random.split(key)
    density = jax.random.randint(level_key, (N_BLK * N_REP, TILE_DEV, 1, 1), 1, 5)
    raw_levels = jax.random.randint(entry_key, (N_BLK * N_REP, TILE_DEV, TS, TS), 0, 16)
    return (raw_levels < density).astype(jnp.int32)


def draw_tile_count(key, part):
    key = jax.random.fold_in(key, 13)
    cut_key, full_key = jax.random.split(key)
    cut_levels = jax.random.randint(cut_key, (N_BLK * N_REP,), 0, 4)
    counts = TILE_DEV - TILE_DEV * cut_levels // 4
    chosen = jax.random.randint(full_key, (), 0, N_BLK * N_REP)
    counts = jnp.where(jnp.arange(N_BLK * N_REP) == chosen, TILE_DEV, counts)
    return counts.astype(jnp.int32)


def block_scale(rng, dims, cuts, smallest, high):
    loudness = 1.0
    for axis_at, parts in cuts:
        draws = jax.random.uniform(jax.random.fold_in(jax.random.fold_in(rng, 6), axis_at), (parts,), jnp.float32, smallest / len(cuts), high / len(cuts))
        loudness = loudness * jnp.repeat(jnp.exp(draws), dims[axis_at] // parts).reshape((-1,) + (1,) * (len(dims) - 1 - axis_at))
    return loudness


def bell_draw(stream_key, extent, deviation, most, shards=(), kind=jnp.bfloat16):
    level = block_scale(stream_key, extent, shards, -0.22, 0.18) if shards else 1.0
    result = jax.random.normal(stream_key, extent, jnp.float32) * deviation * level
    return jnp.minimum(jnp.maximum(result, -most), most).astype(kind)


def setup_inputs(seed: int = 0) -> dict:
    arg_keys = jax.random.split(jax.random.key(seed), 11)
    node_input = bell_draw(arg_keys[0], (NODES, D), 1.0, 6.0, ((0, 256),))
    output_grad = bell_draw(arg_keys[1], (NODES, D), 1.0, 6.0, ((0, 256),))
    saved_output = bell_draw(arg_keys[2], (NODES, D), 0.5, 3.0, ((0, 256),))
    weight_query = bell_draw(arg_keys[3], (D, D), D ** -0.5, 0.1875)
    weight_key = bell_draw(arg_keys[4], (D, D), D ** -0.5, 0.1875)
    weight_value = bell_draw(arg_keys[5], (D, D), D ** -0.5, 0.1875)
    weight_out = bell_draw(arg_keys[6], (D, D), D ** -0.5, 0.1875)
    tile_slots = draw_tile_slots(jax.random.fold_in(arg_keys[10], 71), 0)
    tile_mask = draw_tile_mask(jax.random.fold_in(arg_keys[10], 71), 0)
    tile_count = draw_tile_count(jax.random.fold_in(arg_keys[10], 71), 0)
    return {"node_input": node_input, "output_grad": output_grad, "saved_output": saved_output, "weight_query": weight_query, "weight_key": weight_key, "weight_value": weight_value, "weight_out": weight_out, "tile_slots": tile_slots, "tile_mask": tile_mask, "tile_count": tile_count}


def edge_pass(queries_blk, dout_blk, scale_blk, panels, slot_table, tile_masks, live_count, upper_bound):
    tile_size = tile_masks.shape[-1]
    model_width = queries_blk.shape[1]
    head_size = model_width // HEADS
    per_device = panels.shape[1] // tile_size
    score_scale = head_size ** (-0.5)
    zero_index = jnp.zeros((), jnp.int32)

    def slot_step(slot_index, carried):
        query_acc, band_acc = carried
        row_start = (slot_table[0, slot_index] * tile_size).astype(jnp.int32)
        column_tile = slot_table[1, slot_index]
        band_index = (column_tile // per_device).astype(jnp.int32)
        col_start = (column_tile % per_device * tile_size).astype(jnp.int32)
        tile_queries = lax.dynamic_slice_in_dim(queries_blk, row_start, tile_size, 0).astype(jnp.float32).reshape(tile_size, HEADS, head_size)
        tile_dout = lax.dynamic_slice_in_dim(dout_blk, row_start, tile_size, 0).astype(jnp.float32).reshape(tile_size, HEADS, head_size)
        row_scale = lax.dynamic_slice_in_dim(scale_blk, row_start, tile_size, 0)
        panel = lax.dynamic_slice(panels, (band_index, col_start, zero_index), (1, tile_size, 2 * model_width))[0]
        tile_keys = panel[:, :model_width].astype(jnp.float32).reshape(tile_size, HEADS, head_size)
        tile_values = panel[:, model_width:].astype(jnp.float32).reshape(tile_size, HEADS, head_size)
        live_flag = (slot_index < live_count).astype(jnp.float32)
        edge_mask = tile_masks[slot_index].astype(jnp.float32) * live_flag
        scores = jnp.einsum('ahd,bhd->hab', tile_queries, tile_keys) * score_scale
        gate_vals = jax.nn.sigmoid(scores)
        agreement = jnp.einsum('ahd,bhd->hab', tile_dout, tile_values)
        weights = edge_mask[None] * row_scale[None, :, None] * gate_vals
        edge_probs = weights.astype(jnp.bfloat16).astype(jnp.float32)
        edge_grads = (weights * (1.0 - gate_vals) * agreement * score_scale).astype(jnp.bfloat16).astype(jnp.float32)
        query_tile = jnp.einsum('hab,bhd->ahd', edge_grads, tile_keys).reshape(tile_size, model_width)
        key_tile = jnp.einsum('hab,ahd->bhd', edge_grads, tile_queries).reshape(tile_size, model_width)
        value_tile = jnp.einsum('hab,ahd->bhd', edge_probs, tile_dout).reshape(tile_size, model_width)
        old_rows = lax.dynamic_slice_in_dim(query_acc, row_start, tile_size, 0)
        query_acc = lax.dynamic_update_slice_in_dim(query_acc, old_rows + query_tile, row_start, 0)
        old_band = lax.dynamic_slice(band_acc, (band_index, col_start, zero_index), (1, tile_size, 2 * model_width))
        new_band = old_band + jnp.concatenate([key_tile, value_tile], axis=1)[None]
        band_acc = lax.dynamic_update_slice(band_acc, new_band, (band_index, col_start, zero_index))
        return (query_acc, band_acc)
    initial = (jnp.zeros(queries_blk.shape, jnp.float32), jnp.zeros(panels.shape, jnp.float32))
    return lax.fori_loop(0, upper_bound, slot_step, initial)

def add_rows(target, update, row_start):
    old_rows = lax.dynamic_slice_in_dim(target, row_start, update.shape[0], 0)
    return lax.dynamic_update_slice_in_dim(target, old_rows + update, row_start, 0)

def reference(node_input, output_grad, saved_output, weight_query, weight_key, weight_value, weight_out, tile_slots, tile_mask, tile_count):
    node_count, model_width = node_input.shape
    block_rows = N_REP * R_DEV
    row_tiles = block_rows // TS
    bands = 2 * REACH + 1
    device_count = N_BLK * N_REP
    score_scale = HEAD_DIM ** (-0.5)
    contract_rows = (((1,), (1,)), ((), ()))
    queries = jnp.dot(node_input, weight_query, preferred_element_type=jnp.float32).astype(jnp.bfloat16)
    keys_all = jnp.dot(node_input, weight_key, preferred_element_type=jnp.float32).astype(jnp.bfloat16)
    values_all = jnp.dot(node_input, weight_value, preferred_element_type=jnp.float32).astype(jnp.bfloat16)
    attn_grad = lax.dot_general(output_grad, weight_out, contract_rows, preferred_element_type=jnp.float32).astype(jnp.bfloat16)

    def count_step(degree, device_index):
        blk_index = device_index // N_REP
        live_flag = (jnp.arange(TILE_DEV, dtype=jnp.int32) < tile_count[device_index]).astype(jnp.int32)
        row_sums = lax.optimization_barrier(jnp.sum(tile_mask[device_index], axis=2, dtype=jnp.int32)) * live_flag[:, None]
        picked = (tile_slots[device_index, 0][:, None] == jnp.arange(row_tiles, dtype=jnp.int32)[None, :]).astype(jnp.int32)
        partial_degree = lax.optimization_barrier(jnp.sum(picked[:, :, None] * row_sums[:, None, :], axis=0, dtype=jnp.int32)).reshape(block_rows)
        row_start = (blk_index * block_rows).astype(jnp.int32)
        return (add_rows(degree, partial_degree, row_start), None)
    degree, _ = lax.scan(count_step, jnp.zeros((node_count,), jnp.int32), jnp.arange(device_count, dtype=jnp.int32))
    row_scale = lax.rsqrt(1.0 + degree.astype(jnp.float32))
    kv_all = jnp.concatenate([keys_all, values_all], axis=1)

    def tile_step(carried, device_index):
        query_sum, kv_sum = carried
        blk_index = device_index // N_REP
        rep_index = device_index % N_REP
        row_start = (blk_index * block_rows).astype(jnp.int32)
        queries_blk = lax.dynamic_slice_in_dim(queries, row_start, block_rows, 0)
        dout_blk = lax.dynamic_slice_in_dim(attn_grad, row_start, block_rows, 0)
        scale_blk = lax.dynamic_slice_in_dim(row_scale, row_start, block_rows, 0)
        starts = [(((blk_index + band - REACH) % N_BLK * N_REP + rep_index) * R_DEV).astype(jnp.int32) for band in range(bands)]
        panels = jnp.stack([lax.dynamic_slice_in_dim(kv_all, band_start, R_DEV, 0) for band_start in starts])
        query_part, band_terms = edge_pass(queries_blk, dout_blk, scale_blk, panels, tile_slots[device_index], tile_mask[device_index], tile_count[device_index], TILE_DEV)
        rounded = lax.optimization_barrier(query_part.astype(jnp.bfloat16)).astype(jnp.float32)
        query_sum = add_rows(query_sum, rounded, row_start)
        for band in range(bands):
            kv_sum = add_rows(kv_sum, band_terms[band], starts[band])
        return ((query_sum, kv_sum), None)
    initial = (jnp.zeros((node_count, model_width), jnp.float32), jnp.zeros((node_count, 2 * model_width), jnp.float32))
    (query_sum, kv_sum), _ = lax.scan(tile_step, initial, jnp.arange(device_count, dtype=jnp.int32))
    heads_q = queries.astype(jnp.float32).reshape(node_count, HEADS, HEAD_DIM)
    heads_k = keys_all.astype(jnp.float32).reshape(node_count, HEADS, HEAD_DIM)
    heads_v = values_all.astype(jnp.float32).reshape(node_count, HEADS, HEAD_DIM)
    heads_g = attn_grad.astype(jnp.float32).reshape(node_count, HEADS, HEAD_DIM)
    self_gate = jax.nn.sigmoid(lax.optimization_barrier(jnp.sum(heads_q * heads_k, axis=-1)) * score_scale)
    self_agree = lax.optimization_barrier(jnp.sum(heads_g * heads_v, axis=-1))
    self_edge = row_scale[:, None] * self_gate * (1.0 - self_gate) * self_agree * score_scale
    d_query = (query_sum + (self_edge[..., None] * heads_k).reshape(node_count, model_width)).astype(jnp.bfloat16)
    d_key = (kv_sum[:, :model_width] + (self_edge[..., None] * heads_q).reshape(node_count, model_width)).astype(jnp.bfloat16)
    d_value = (kv_sum[:, model_width:] + ((row_scale[:, None] * self_gate)[..., None] * heads_g).reshape(node_count, model_width)).astype(jnp.bfloat16)
    input_grad = lax.dot_general(d_query, weight_query, contract_rows, preferred_element_type=jnp.float32)
    input_grad = input_grad + lax.dot_general(d_key, weight_key, contract_rows, preferred_element_type=jnp.float32)
    input_grad = input_grad + lax.dot_general(d_value, weight_value, contract_rows, preferred_element_type=jnp.float32)
    input_grad = input_grad.astype(jnp.bfloat16)

    def block_grads(blk_index):
        totals = jnp.zeros((model_width, 4 * model_width), jnp.float32)
        for rep_index in range(N_REP):
            row_start = ((blk_index * N_REP + rep_index) * R_DEV).astype(jnp.int32)
            pieces = []
            for source, gradient in ((node_input, d_query), (node_input, d_key), (node_input, d_value), (saved_output, output_grad)):
                source_rows = lax.dynamic_slice_in_dim(source, row_start, R_DEV, 0)
                gradient_rows = lax.dynamic_slice_in_dim(gradient, row_start, R_DEV, 0)
                pieces.append(lax.dot_general(source_rows, gradient_rows, (((0,), (0,)), ((), ())), preferred_element_type=jnp.float32))
            device_term = jnp.concatenate(pieces, axis=1)
            totals = totals + lax.optimization_barrier(device_term.astype(jnp.bfloat16)).astype(jnp.float32)
        return totals.astype(jnp.bfloat16)
    stacked = lax.map(block_grads, jnp.arange(N_BLK, dtype=jnp.int32))
    return (input_grad, stacked[:, :, :model_width], stacked[:, :, model_width:2 * model_width], stacked[:, :, 2 * model_width:3 * model_width], stacked[:, :, 3 * model_width:])
```

```python
import functools

import jax
import jax.numpy as jnp
from jax import lax
from jax.experimental import pallas as pl
from jax.experimental.pallas import tpu as pltpu
from jax.sharding import PartitionSpec as P

HEADS = 16
HEAD_DIM = 64
PARTS = 2


def moved(shard, to_blk=lambda b: b, to_rep=lambda r: r):
    n_blk, n_rep = lax.axis_size("blk"), lax.axis_size("rep")
    pairs = [
        (b * n_rep + r, to_blk(b) % n_blk * n_rep + to_rep(r))
        for b in range(n_blk)
        for r in range(n_rep)
    ]
    return lax.ppermute(shard, ("blk", "rep"), pairs)


def to_core(shard):
    return moved(shard, to_rep=lambda r: r ^ 1)


def to_partner(shard):
    return moved(shard, to_rep=lambda r: r ^ 2)


def to_cross(shard):
    return moved(shard, to_blk=lambda b: b ^ 1, to_rep=lambda r: r ^ 2)


def to_flip(shard):
    return moved(shard, to_blk=lambda b: b ^ 1)


def to_up(shard):
    return moved(shard, to_blk=lambda b: b - 2)


def to_down(shard):
    return moved(shard, to_blk=lambda b: b + 2)


def to_outer(shard):
    return moved(shard, to_blk=lambda b: b + 2 if b % 2 == 0 else b - 2)


def to_inner(shard):
    return moved(shard, to_blk=lambda b: b - 2 if b % 2 == 0 else b + 2)


NT = (((1,), (1,)), ((), ()))
NN = (((1,), (0,)), ((), ()))
TN = (((0,), (0,)), ((), ()))


def mm(a, b, dims=NN):
    return lax.dot_general(a, b, dims, preferred_element_type=jnp.float32)


def edge_kernel(n_row, n_band, width, col, slots, count, scale, mask, own_scale, *refs):
    ins, refs = refs[: 2 * n_row + 2 * n_band], refs[2 * n_row + 2 * n_band :]
    q_in, g_in = ins[:n_row], ins[n_row : 2 * n_row]
    k_in, v_in = ins[2 * n_row : 2 * n_row + n_band], ins[2 * n_row + n_band :]
    out_near, out_far, out_own, out_flip, out_up, out_down, out_diag = refs[:7]
    q_all, g_all, k_all, v_all, q_acc, k_acc, v_acc, sems = refs[7:]
    own_rows = k_in[0].shape[0]
    tile = mask.shape[-1]
    cols = pl.ds(col, width)
    copies = []
    for pieces, target in ((q_in, q_all), (g_in, g_all), (k_in, k_all), (v_in, v_all)):
        for at, piece in enumerate(pieces):
            copies.append(
                pltpu.make_async_copy(
                    piece.at[:, cols],
                    target.at[pl.ds(at * own_rows, own_rows), :],
                    sems.at[len(copies)],
                )
            )
    for copy in copies:
        copy.start()
    for acc in (q_acc, k_acc, v_acc):
        acc[own_rows:, :] = jnp.zeros((acc.shape[0] - own_rows, width), jnp.float32)
    for copy in copies:
        copy.wait()

    low = lax.broadcasted_iota(jnp.int32, (tile, tile), 1) < HEAD_DIM
    same_head = (lax.broadcasted_iota(jnp.int32, (tile, tile), 0) < HEAD_DIM) == low
    ones = same_head.astype(jnp.float32).astype(jnp.bfloat16)

    def split(part):
        zero = jnp.zeros_like(part)
        return jnp.concatenate([jnp.where(low, part, zero), jnp.where(low, zero, part)], axis=0)

    def head_sums(a, b):
        product = a * b
        head = product.astype(jnp.bfloat16)
        tail = (product - head.astype(jnp.float32)).astype(jnp.bfloat16)
        return mm(head, ones) + mm(tail, ones)

    for pair in range(width // tile):
        here = slice(pair * tile, (pair + 1) * tile)
        q, g, k, v = (
            ref[:own_rows, here].astype(jnp.float32) for ref in (q_all, g_all, k_all, v_all)
        )
        gate = jax.nn.sigmoid(head_sums(q, k) * HEAD_DIM**-0.5)
        weight = own_scale[...] * gate
        edge = weight * (1.0 - gate) * head_sums(g, v) * HEAD_DIM**-0.5
        q_acc[:own_rows, here] = edge * k
        k_acc[:own_rows, here] = edge * q
        v_acc[:own_rows, here] = weight * g

    def slot_step(slot, _):
        row_tile = slots[0, slot]
        rows = pl.ds(pl.multiple_of(row_tile * tile, tile), tile)
        band = pl.ds(pl.multiple_of(slots[1, slot] * tile, tile), tile)
        edge = mask[slot].astype(jnp.float32).T * scale[pl.ds(row_tile, 1), :]
        edge = jnp.concatenate([edge, edge], axis=1)
        for pair in range(width // tile):
            here = slice(pair * tile, (pair + 1) * tile)
            keys, values = k_all[band, here], v_all[band, here]
            queries, grads = split(q_all[rows, here]), split(g_all[rows, here])
            score = mm(keys, queries, NT)
            agree = mm(values, grads, NT)
            gate = 0.5 * jnp.tanh(score * (0.5 * HEAD_DIM**-0.5)) + 0.5
            weight = edge * gate
            prob = weight.astype(jnp.bfloat16)
            grad = (weight * (1.0 - gate) * (agree * HEAD_DIM**-0.5)).astype(jnp.bfloat16)
            k_acc[band, here] += mm(grad, queries)
            v_acc[band, here] += mm(prob, grads)
            flat = jnp.concatenate([grad[:, :tile].T, grad[:, tile:].T], axis=1)
            q_acc[rows, here] += mm(flat, split(keys))
        return 0

    lax.fori_loop(0, count[0], slot_step, 0)
    near = out_near.shape[0]
    out_near[...] = q_acc[:near, :]
    out_far[...] = q_acc[near:, :].astype(jnp.bfloat16)
    for i, out in enumerate((out_own, out_up, out_down, out_flip, out_diag)):
        here = slice(i * own_rows, (i + 1) * own_rows)
        out[:, :width] = k_acc[here, :].astype(out.dtype)
        out[:, width:] = v_acc[here, :].astype(out.dtype)


def edge_pass(slots, count, scale, mask, own_scale, q, g, k, v, col, width):
    n_row, n_band, own_rows = len(q), len(k), k[0].shape[0]
    q_rows, band_rows = n_row * own_rows, n_band * own_rows
    vmem = pl.BlockSpec(memory_space=pltpu.VMEM)
    smem = pl.BlockSpec(memory_space=pltpu.SMEM)
    anywhere = pl.BlockSpec(memory_space=pl.ANY)
    pieces = (*q, *g, *k, *v)
    term = jax.ShapeDtypeStruct((own_rows, 2 * width), jnp.bfloat16)
    term_wide = jax.ShapeDtypeStruct((own_rows, 2 * width), jnp.float32)
    return pl.pallas_call(
        functools.partial(edge_kernel, n_row, n_band, width, col),
        out_shape=[
            jax.ShapeDtypeStruct((q_rows // 2, width), jnp.float32),
            jax.ShapeDtypeStruct((q_rows // 2, width), jnp.bfloat16),
            term_wide,
            term_wide,
            term,
            term,
            term,
        ],
        in_specs=[smem, smem, vmem, vmem, vmem] + [anywhere] * len(pieces),
        out_specs=[vmem] * 7,
        scratch_shapes=[
            pltpu.VMEM((q_rows, width), jnp.bfloat16),
            pltpu.VMEM((q_rows, width), jnp.bfloat16),
            pltpu.VMEM((band_rows, width), jnp.bfloat16),
            pltpu.VMEM((band_rows, width), jnp.bfloat16),
            pltpu.VMEM((q_rows, width), jnp.float32),
            pltpu.VMEM((band_rows, width), jnp.float32),
            pltpu.VMEM((band_rows, width), jnp.float32),
            pltpu.SemaphoreType.DMA((len(pieces),)),
        ],
        compiler_params=pltpu.CompilerParams(vmem_limit_bytes=48 * 2**20),
        cost_estimate=pl.CostEstimate(
            flops=170 * mask.size * width,
            bytes_accessed=12 * band_rows * width,
            transcendentals=mask.size * width // HEAD_DIM,
        ),
        name="edges",
    )(slots, count, scale, mask, own_scale, *pieces)


def on_device(
    node_input,
    output_grad,
    saved_output,
    weight_query,
    weight_key,
    weight_value,
    weight_out,
    tile_slots,
    tile_mask,
    tile_count,
):
    bf16, f32 = jnp.bfloat16, jnp.float32
    own_rows, model_width = node_input.shape
    rep = lax.axis_index("rep")
    blk = lax.axis_index("blk")
    masks = tile_mask[0]
    n_slot, tile = masks.shape[0], masks.shape[-1]
    per_group = own_rows // tile
    n_rep = lax.axis_size("rep")

    group = tile_slots[0, 0] // per_group ^ rep
    place = (group >> 1) | ((group & 1) << 1)
    row_tile = place * per_group + tile_slots[0, 0] % per_group
    band = tile_slots[0, 1] // per_group
    odd = blk % 2
    band_place = jnp.where(
        band == 2,
        0,
        jnp.where(
            band == 0, 1, jnp.where(band == 4, 2, jnp.where((band == 3) == (odd == 0), 3, 4))
        ),
    )
    slots = jnp.stack([row_tile, band_place * per_group + tile_slots[0, 1] % per_group])

    live = (jnp.arange(n_slot, dtype=jnp.int32) < tile_count[0]).astype(jnp.int32)
    row_sums = jnp.sum(masks, axis=2, dtype=jnp.int32) * live[:, None]
    picked = (
        row_tile[:, None] == jnp.arange(n_rep * per_group, dtype=jnp.int32)[None, :]
    ).astype(jnp.int32)
    degree = jnp.sum(picked[:, :, None] * row_sums[:, None, :], axis=0, dtype=jnp.int32)
    other = to_core(degree).reshape(2, 2 * per_group, tile)
    degree = degree + other[::-1].reshape(degree.shape)
    other = to_partner(degree).reshape(2, 2, per_group, tile)
    degree = degree + other[:, ::-1].reshape(degree.shape)
    scale = lax.rsqrt(1.0 + degree.astype(f32))
    own_scale = scale[:per_group].reshape(own_rows, 1)

    x_partner = to_partner(node_input)
    x_up = to_down(node_input)
    x_down = to_up(node_input)
    x_flip = to_cross(x_partner)
    y_partner = to_partner(output_grad)
    x_diag = to_outer(x_flip)
    x_rows = [node_input, x_partner, to_core(node_input), to_core(x_partner)]
    y_rows = [output_grad, y_partner, to_core(output_grad), to_core(y_partner)]
    bands = [node_input, x_up, x_down, x_flip, x_diag]

    queries = [mm(x, weight_query).astype(bf16) for x in x_rows]
    grads = [mm(y, weight_out, NT).astype(bf16) for y in y_rows]
    keys = [mm(x, weight_key).astype(bf16) for x in bands]
    values = [mm(x, weight_value).astype(bf16) for x in bands]

    quarter = model_width // n_rep

    def quarter_of(array, which):
        return lax.dynamic_slice_in_dim(array, which * quarter, quarter, 1)

    core, chip = rep % 2, rep // 2
    s_partner = to_partner(
        lax.dynamic_slice_in_dim(saved_output, (1 - chip) * 2 * quarter, 2 * quarter, 1)
    )
    s_cols = [
        quarter_of(saved_output, rep),
        quarter_of(s_partner, core),
        to_core(quarter_of(saved_output, rep ^ 1)),
        to_core(quarter_of(s_partner, 1 - core)),
    ]
    x_cols = [quarter_of(x, rep) for x in x_rows]

    def weight_grad(sources, gradients):
        total = mm(sources[0], gradients[0], TN)
        for source, gradient in zip(sources[1:], gradients[1:]):
            total = total + mm(source, gradient, TN)
        return total.astype(bf16)

    def all_rows(own):
        partner = to_partner(own)
        return [own, partner, to_core(own), to_core(partner)]

    out_weight_grad = weight_grad(s_cols, y_rows)

    width = model_width // PARTS
    input_grad = 0.0
    query_grads, key_grads, value_grads = [], [], []
    for part in range(PARTS):
        cols = slice(part * width, (part + 1) * width)
        near, far, own, flip, up, down, diag = edge_pass(
            slots, tile_count, scale, masks, own_scale, queries, grads, keys, values,
            part * width, width,
        )
        inner = to_inner(diag)
        near = near + to_core(far).astype(f32)
        up, down = to_up(up), to_down(down)
        flip = to_flip((flip + inner.astype(f32)).astype(bf16))
        d_query = (
            near[:own_rows] + to_partner(near[own_rows:].astype(bf16)).astype(f32)
        ).astype(bf16)
        d_kv = (own + up.astype(f32) + down.astype(f32) + flip.astype(f32)).astype(bf16)
        query_grads.append(weight_grad(x_cols, all_rows(d_query)))
        kv_grad = weight_grad(x_cols, all_rows(d_kv))
        key_grads.append(kv_grad[:, :width])
        value_grads.append(kv_grad[:, width:])
        input_grad = input_grad + mm(d_query, weight_query[:, cols], NT)
        input_grad = input_grad + mm(d_kv[:, :width], weight_key[:, cols], NT)
        input_grad = input_grad + mm(d_kv[:, width:], weight_value[:, cols], NT)

    def joined(pieces):
        return jnp.concatenate(pieces, axis=1)[None]

    return (
        input_grad.astype(bf16),
        joined(query_grads),
        joined(key_grads),
        joined(value_grads),
        out_weight_grad[None],
    )


def solution(mesh):
    placed = (
        P(("blk", "rep"), None),
        P(("blk", "rep"), None),
        P(("blk", "rep"), None),
        P(),
        P(),
        P(),
        P(),
        P(("blk", "rep"), None, None),
        P(("blk", "rep"), None, None, None),
        P(("blk", "rep")),
    )
    return jax.shard_map(
        on_device,
        mesh=mesh,
        in_specs=placed,
        out_specs=(
            P(("blk", "rep"), None),
            P("blk", "rep", None),
            P("blk", "rep", None),
            P("blk", "rep", None),
            P("blk", "rep", None),
        ),
        check_vma=False,
    )
```

```python
import functools

import jax
import jax.numpy as jnp
from jax import lax
from jax.experimental import pallas as pl
from jax.experimental.pallas import tpu as pltpu
from jax.sharding import PartitionSpec as P

HEADS = 16
HEAD_DIM = 64
PARTS = 2


def moved(shard, to_blk=lambda b: b, to_rep=lambda r: r):
    n_blk, n_rep = lax.axis_size("blk"), lax.axis_size("rep")
    pairs = [
        (b * n_rep + r, to_blk(b) % n_blk * n_rep + to_rep(r))
        for b in range(n_blk)
        for r in range(n_rep)
    ]
    return lax.ppermute(shard, ("blk", "rep"), pairs)


def to_core(shard):
    return moved(shard, to_rep=lambda r: r ^ 1)


def to_partner(shard):
    return moved(shard, to_rep=lambda r: r ^ 2)


def to_cross(shard):
    return moved(shard, to_blk=lambda b: b ^ 1, to_rep=lambda r: r ^ 2)


def to_flip(shard):
    return moved(shard, to_blk=lambda b: b ^ 1)


def to_outer(shard):
    return moved(shard, to_blk=lambda b: b + 2 if b % 2 == 0 else b - 2)


def to_inner(shard):
    return moved(shard, to_blk=lambda b: b - 2 if b % 2 == 0 else b + 2)


def after(value, *earlier):
    return lax.optimization_barrier((value, *earlier))[0]


NT = (((1,), (1,)), ((), ()))
NN = (((1,), (0,)), ((), ()))
TN = (((0,), (0,)), ((), ()))


def mm(a, b, dims=NN):
    return lax.dot_general(a, b, dims, preferred_element_type=jnp.float32)


def project_kernel(jobs, n_x, n_w, *refs):
    xs, ws, outs = refs[:n_x], refs[n_x : n_x + n_w], refs[n_x + n_w :]
    for (x, w, dims), out in zip(jobs, outs):
        out[...] = mm(xs[x][...], ws[w][...], dims).astype(out.dtype)


def project(xs, ws, jobs):
    rows, depth = xs[0].shape
    wide = 256
    steps = depth // wide
    whole = pl.BlockSpec((rows, depth), lambda i: (0, 0))
    transposed = {w: dims == NT for _, w, dims in jobs}
    return pl.pallas_call(
        functools.partial(project_kernel, jobs, len(xs), len(ws)),
        grid=(steps,),
        in_specs=[whole] * len(xs)
        + [
            pl.BlockSpec((wide, depth), lambda i: (i, 0))
            if transposed[w]
            else pl.BlockSpec((depth, wide), lambda i: (0, i))
            for w in range(len(ws))
        ],
        out_specs=[pl.BlockSpec((rows, wide), lambda i: (0, i))] * len(jobs),
        out_shape=[jax.ShapeDtypeStruct((rows, depth), jnp.bfloat16)] * len(jobs),
        compiler_params=pltpu.CompilerParams(vmem_limit_bytes=63 * 2**20),
        cost_estimate=pl.CostEstimate(
            flops=3 * len(jobs) * rows * depth * depth,
            bytes_accessed=2 * depth * (len(xs) * rows + len(ws) * depth + len(jobs) * rows),
            transcendentals=0,
        ),
        name="project",
    )(*xs, *ws)


def transpose_kernel(which, *refs):
    rows = refs[0].shape[0]
    for i, piece in enumerate(refs[:-1]):
        refs[-1][:, i * rows : (i + 1) * rows] = piece[...].T


def transposed_columns(which, pieces, wide):
    rows = pieces[0].shape[0]
    blocks = which.shape[0]
    return pl.pallas_call(
        transpose_kernel,
        grid_spec=pltpu.PrefetchScalarGridSpec(
            num_scalar_prefetch=1,
            grid=(blocks,),
            in_specs=[pl.BlockSpec((rows, wide), lambda i, which: (0, which[i]))] * len(pieces),
            out_specs=pl.BlockSpec((wide, rows * len(pieces)), lambda i, which: (i, 0)),
        ),
        out_shape=jax.ShapeDtypeStruct((blocks * wide, rows * len(pieces)), jnp.bfloat16),
        compiler_params=pltpu.CompilerParams(vmem_limit_bytes=16 * 2**20),
        cost_estimate=pl.CostEstimate(
            flops=10**9, bytes_accessed=4 * blocks * wide * rows * len(pieces), transcendentals=0
        ),
        name="transposed_columns",
    )(which, *pieces)


def weight_grad_kernel(n_set, n_step, x_cols, *refs):
    sets, (mine, theirs) = refs[:-2], refs[-2:]
    size = len(sets) // n_set
    half = mine.shape[0]
    step = pl.program_id(0)
    for which in range(n_set):

        @pl.when((step >= which * n_step) & (step < (which + 1) * n_step))
        def _():
            total = jnp.zeros((2 * half, mine.shape[1]), jnp.float32)
            at = 0
            for piece in sets[which * size : (which + 1) * size]:
                rows = piece.shape[0]
                total = total + mm(x_cols[:, at : at + rows], piece[...])
                at += rows
            mine[...] = total[:half]
            theirs[...] = total[half:].astype(theirs.dtype)


def weight_grads(x_cols, *sets):
    width = sets[0][0].shape[1]
    wide = 256
    n_step = width // wide
    half, depth = x_cols.shape[0] // 2, x_cols.shape[1]

    def columns(which):
        return lambda i: (0, jnp.clip(i - which * n_step, 0, n_step - 1))

    return pl.pallas_call(
        functools.partial(weight_grad_kernel, len(sets), n_step),
        grid=(len(sets) * n_step,),
        in_specs=[pl.BlockSpec((2 * half, depth), lambda i: (0, 0))]
        + [
            pl.BlockSpec((piece.shape[0], wide), columns(which))
            for which, pieces in enumerate(sets)
            for piece in pieces
        ],
        out_specs=[pl.BlockSpec((half, wide), lambda i: (0, i))] * 2,
        out_shape=[
            jax.ShapeDtypeStruct((half, len(sets) * width), jnp.float32),
            jax.ShapeDtypeStruct((half, len(sets) * width), jnp.bfloat16),
        ],
        compiler_params=pltpu.CompilerParams(vmem_limit_bytes=16 * 2**20),
        cost_estimate=pl.CostEstimate(
            flops=8 * half * depth * width * len(sets),
            bytes_accessed=2 * depth * (2 * half + width) + 6 * half * width,
            transcendentals=0,
        ),
        name="weight_grads",
    )(x_cols, *(piece for pieces in sets for piece in pieces))


def edge_kernel(n_row, n_band, width, col, slots, count, scale, mask, own_scale, *refs):
    ins, refs = refs[: 2 * n_row + 2 * n_band], refs[2 * n_row + 2 * n_band :]
    q_in, g_in = ins[:n_row], ins[n_row : 2 * n_row]
    k_in, v_in = ins[2 * n_row : 2 * n_row + n_band], ins[2 * n_row + n_band :]
    out_near, out_far, out_own, out_flip, out_side, out_back, out_diag = refs[:7]
    q_all, g_all, k_all, v_all, q_acc, k_acc, v_acc, sems = refs[7:]
    own_rows = k_in[0].shape[0]
    tile = mask.shape[-1]
    cols = pl.ds(col, width)
    copies = []
    for pieces, target in ((q_in, q_all), (g_in, g_all), (k_in, k_all), (v_in, v_all)):
        for at, piece in enumerate(pieces):
            copies.append(
                pltpu.make_async_copy(
                    piece.at[:, cols],
                    target.at[pl.ds(at * own_rows, own_rows), :],
                    sems.at[len(copies)],
                )
            )
    for copy in copies:
        copy.start()
    for acc in (q_acc, k_acc, v_acc):
        acc[own_rows:, :] = jnp.zeros((acc.shape[0] - own_rows, width), jnp.float32)
    for copy in copies:
        copy.wait()

    low = lax.broadcasted_iota(jnp.int32, (tile, tile), 1) < HEAD_DIM
    same_head = (lax.broadcasted_iota(jnp.int32, (tile, tile), 0) < HEAD_DIM) == low
    ones = same_head.astype(jnp.float32).astype(jnp.bfloat16)

    def split(part):
        zero = jnp.zeros_like(part)
        return jnp.concatenate([jnp.where(low, part, zero), jnp.where(low, zero, part)], axis=0)

    def head_sums(a, b):
        product = a * b
        head = product.astype(jnp.bfloat16)
        tail = (product - head.astype(jnp.float32)).astype(jnp.bfloat16)
        return mm(head, ones) + mm(tail, ones)

    for pair in range(width // tile):
        here = slice(pair * tile, (pair + 1) * tile)
        q, g, k, v = (
            ref[:own_rows, here].astype(jnp.float32) for ref in (q_all, g_all, k_all, v_all)
        )
        gate = jax.nn.sigmoid(head_sums(q, k) * HEAD_DIM**-0.5)
        weight = own_scale[...] * gate
        edge = weight * (1.0 - gate) * head_sums(g, v) * HEAD_DIM**-0.5
        q_acc[:own_rows, here] = edge * k
        k_acc[:own_rows, here] = edge * q
        v_acc[:own_rows, here] = weight * g

    def slot_step(slot, _):
        row_tile = slots[0, slot]
        rows = pl.ds(pl.multiple_of(row_tile * tile, tile), tile)
        band = pl.ds(pl.multiple_of(slots[1, slot] * tile, tile), tile)
        edge = mask[slot].astype(jnp.float32).T * scale[pl.ds(row_tile, 1), :]
        edge = jnp.concatenate([edge, edge], axis=1)
        for pair in range(width // tile):
            here = slice(pair * tile, (pair + 1) * tile)
            keys, values = k_all[band, here], v_all[band, here]
            queries, grads = split(q_all[rows, here]), split(g_all[rows, here])
            score = mm(keys, queries, NT)
            agree = mm(values, grads, NT)
            gate = 0.5 * jnp.tanh(score * (0.5 * HEAD_DIM**-0.5)) + 0.5
            weight = edge * gate
            prob = weight.astype(jnp.bfloat16)
            grad = (weight * (1.0 - gate) * (agree * HEAD_DIM**-0.5)).astype(jnp.bfloat16)
            k_acc[band, here] += mm(grad, queries)
            v_acc[band, here] += mm(prob, grads)
            flat = jnp.concatenate([grad[:, :tile].T, grad[:, tile:].T], axis=1)
            q_acc[rows, here] += mm(flat, split(keys))
        return 0

    lax.fori_loop(0, count[0], slot_step, 0)
    near = out_near.shape[0]
    out_near[...] = q_acc[:near, :]
    out_far[...] = q_acc[near:, :].astype(jnp.bfloat16)
    for i, out in enumerate((out_own, out_side, out_back, out_flip, out_diag)):
        here = slice(i * own_rows, (i + 1) * own_rows)
        out[:, :width] = k_acc[here, :].astype(out.dtype)
        out[:, width:] = v_acc[here, :].astype(out.dtype)


def edge_pass(slots, count, scale, mask, own_scale, q, g, k, v, col, width):
    n_row, n_band, own_rows = len(q), len(k), k[0].shape[0]
    q_rows, band_rows = n_row * own_rows, n_band * own_rows
    vmem = pl.BlockSpec(memory_space=pltpu.VMEM)
    smem = pl.BlockSpec(memory_space=pltpu.SMEM)
    anywhere = pl.BlockSpec(memory_space=pl.ANY)
    pieces = (*q, *g, *k, *v)
    term = jax.ShapeDtypeStruct((own_rows, 2 * width), jnp.bfloat16)
    term_wide = jax.ShapeDtypeStruct((own_rows, 2 * width), jnp.float32)
    return pl.pallas_call(
        functools.partial(edge_kernel, n_row, n_band, width, col),
        out_shape=[
            jax.ShapeDtypeStruct((q_rows // 2, width), jnp.float32),
            jax.ShapeDtypeStruct((q_rows // 2, width), jnp.bfloat16),
            term_wide,
            term_wide,
            term,
            term,
            term,
        ],
        in_specs=[smem, smem, vmem, vmem, vmem] + [anywhere] * len(pieces),
        out_specs=[vmem] * 7,
        scratch_shapes=[
            pltpu.VMEM((q_rows, width), jnp.bfloat16),
            pltpu.VMEM((q_rows, width), jnp.bfloat16),
            pltpu.VMEM((band_rows, width), jnp.bfloat16),
            pltpu.VMEM((band_rows, width), jnp.bfloat16),
            pltpu.VMEM((q_rows, width), jnp.float32),
            pltpu.VMEM((band_rows, width), jnp.float32),
            pltpu.VMEM((band_rows, width), jnp.float32),
            pltpu.SemaphoreType.DMA((len(pieces),)),
        ],
        compiler_params=pltpu.CompilerParams(vmem_limit_bytes=32 * 2**20),
        cost_estimate=pl.CostEstimate(
            flops=mask.size * width, bytes_accessed=band_rows * width, transcendentals=0
        ),
        name="edges",
    )(slots, count, scale, mask, own_scale, *pieces)


def on_device(
    node_input,
    output_grad,
    saved_output,
    weight_query,
    weight_key,
    weight_value,
    weight_out,
    tile_slots,
    tile_mask,
    tile_count,
):
    bf16, f32 = jnp.bfloat16, jnp.float32
    own_rows, model_width = node_input.shape
    rep = lax.axis_index("rep")
    blk = lax.axis_index("blk")
    masks = tile_mask[0]
    n_slot, tile = masks.shape[0], masks.shape[-1]
    per_group = own_rows // tile
    n_rep = lax.axis_size("rep")

    group = tile_slots[0, 0] // per_group ^ rep
    place = (group >> 1) | ((group & 1) << 1)
    row_tile = place * per_group + tile_slots[0, 0] % per_group
    band = tile_slots[0, 1] // per_group
    offset = jnp.where(blk % 2 == 0, band - 2, 2 - band)
    band_place = jnp.where(
        offset == 0,
        0,
        jnp.where(offset == -2, 1, jnp.where(offset == 2, 2, jnp.where(offset == 1, 3, 4))),
    )
    slots = jnp.stack([row_tile, band_place * per_group + tile_slots[0, 1] % per_group])

    x_partner = to_partner(node_input)
    x_side = to_outer(node_input)
    x_back = to_inner(node_input)

    live = (jnp.arange(n_slot, dtype=jnp.int32) < tile_count[0]).astype(jnp.int32)
    row_sums = jnp.sum(masks, axis=2, dtype=jnp.int32) * live[:, None]
    picked = (
        row_tile[:, None] == jnp.arange(n_rep * per_group, dtype=jnp.int32)[None, :]
    ).astype(jnp.int32)
    degree = jnp.sum(picked[:, :, None] * row_sums[:, None, :], axis=0, dtype=jnp.int32)
    other = to_core(degree).reshape(2, 2 * per_group, tile)
    degree = degree + other[::-1].reshape(degree.shape)
    x_flip = to_cross(x_partner)
    x_cores = to_core(after(node_input, x_partner)), to_core(x_partner)
    y_partner = to_partner(after(output_grad, x_partner))
    k_near = project(
        [after(node_input, x_partner, *x_cores), x_side, x_back],
        [weight_key, weight_value],
        [(x, w, NN) for w in range(2) for x in range(3)],
    )
    x_diag = to_outer(after(x_flip, k_near[0]))
    other = to_partner(after(degree, y_partner)).reshape(2, 2, per_group, tile)
    degree = degree + other[:, ::-1].reshape(degree.shape)
    scale = lax.rsqrt(1.0 + degree.astype(f32))
    own_scale = scale[:per_group].reshape(own_rows, 1)
    y_cores = to_core(after(output_grad, y_partner, k_near[0])), to_core(after(y_partner, k_near[0]))
    x_rows = [node_input, x_partner, *x_cores]
    y_rows = [output_grad, y_partner, *y_cores]
    middle = project(
        [*x_rows, x_flip, *y_rows],
        [weight_query, weight_out, weight_key, weight_value],
        [(x, 0, NN) for x in range(4)] + [(x, 1, NT) for x in range(5, 9)]
        + [(4, 2, NN), (4, 3, NN)],
    )
    queries, grads = middle[:4], middle[4:8]
    quarter = model_width // n_rep

    def quarter_of(array, which):
        return lax.dynamic_slice_in_dim(array, which * quarter, quarter, 1)

    core, chip = rep % 2, rep // 2
    s_partner = to_partner(
        lax.dynamic_slice_in_dim(
            after(saved_output, y_cores[1]), (1 - chip) * 2 * quarter, 2 * quarter, 1
        )
    )
    s_cols = [
        quarter_of(saved_output, rep),
        quarter_of(s_partner, core),
        to_core(quarter_of(after(saved_output, s_partner), rep ^ 1)),
        to_core(quarter_of(s_partner, 1 - core)),
    ]
    x_cols = transposed_columns(jnp.stack([rep, rep ^ 2]), x_rows, quarter)

    def weight_grad(sources, gradients):
        total = mm(sources[0], gradients[0], TN)
        for source, gradient in zip(sources[1:], gradients[1:]):
            total = total + mm(source, gradient, TN)
        return total

    def summed(*sets):
        mine, theirs = weight_grads(x_cols, *sets)
        return (mine + to_partner(theirs).astype(f32)).astype(bf16), theirs

    out_weight_grad = weight_grad(s_cols, y_rows).astype(bf16)
    x_diag = after(x_diag, x_cols, *s_cols[2:])
    keys = [*k_near[:3], middle[8], mm(x_diag, weight_key).astype(bf16)]
    values = [*k_near[3:], middle[9], mm(x_diag, weight_value).astype(bf16)]

    width = model_width // PARTS

    def edges(part, *gate):
        return edge_pass(
            after(slots, *gate), tile_count, scale, masks, own_scale, queries, grads, keys,
            values, part * width, width,
        )

    def chip_terms(near, far):
        near = (near + to_core(far).astype(f32)).astype(bf16)
        return near, to_core(near)

    def crossed(flip, inner):
        return to_cross((flip + inner.astype(f32)).astype(bf16))

    def finish(part, totals, near, own, side, back, foreign):
        cols = slice(part * width, (part + 1) * width)
        w_query = weight_query[:, cols]
        w_key, w_value = weight_key[:, cols], weight_value[:, cols]
        kv = (own + side.astype(f32) + back.astype(f32)).astype(bf16)
        both = jnp.concatenate([kv, foreign], axis=0)
        totals = [
            total
            + mm(q, w_query, NT)
            + mm(terms[:, :width], w_key, NT)
            + mm(terms[:, width:], w_value, NT)
            for total, q, terms in (
                (totals[0], near[:own_rows], kv),
                (totals[1], near[own_rows:], foreign),
            )
        ]
        return totals, *summed([both, to_core(both)])

    near_0, far_0, own_0, flip_0, side_0, back_0, diag_0 = edges(0)
    q_0 = chip_terms(near_0, far_0)
    inner_0, side_0, back_0 = to_inner(diag_0), to_inner(side_0), to_outer(back_0)
    near_1, far_1, own_1, flip_1, side_1, back_1, diag_1 = edges(1, q_0[0], out_weight_grad)
    q_1 = chip_terms(near_1, far_1)
    own_0, flip_0 = after((own_0, flip_0), far_1)
    cross_0 = crossed(flip_0, inner_0)
    inner_1 = to_inner(after(diag_1, inner_0))
    query_grad, q_sent = summed(q_0, q_1)
    cross_1 = crossed(after(flip_1, q_sent), inner_1)
    totals, kv_grad_0, kv_sent = finish(
        0, (0.0, 0.0), q_0[0], own_0, side_0, back_0, after(cross_0, q_sent)
    )
    side_1, back_1 = after((side_1, back_1), inner_1, query_grad, kv_sent)
    side_1, back_1 = to_inner(side_1), to_outer(back_1)
    totals, kv_grad_1, _ = finish(
        1, totals, q_1[0], own_1, side_1, back_1, after(cross_1, kv_sent)
    )
    grad_partner = to_partner(after(totals[1], kv_grad_0).astype(bf16))
    input_grad = totals[0] + grad_partner.astype(f32)
    key_grads = [grad[:, :width] for grad in (kv_grad_0, kv_grad_1)]
    value_grads = [grad[:, width:] for grad in (kv_grad_0, kv_grad_1)]

    def joined(pieces):
        return jnp.concatenate(pieces, axis=1)[None]

    return (
        input_grad.astype(bf16),
        query_grad[None],
        joined(key_grads),
        joined(value_grads),
        out_weight_grad[None],
    )


def solution(mesh):
    placed = (
        P(("blk", "rep"), None),
        P(("blk", "rep"), None),
        P(("blk", "rep"), None),
        P(),
        P(),
        P(),
        P(),
        P(("blk", "rep"), None, None),
        P(("blk", "rep"), None, None, None),
        P(("blk", "rep")),
    )
    return jax.shard_map(
        on_device,
        mesh=mesh,
        in_specs=placed,
        out_specs=(
            P(("blk", "rep"), None),
            P("blk", "rep", None),
            P("blk", "rep", None),
            P("blk", "rep", None),
            P("blk", "rep", None),
        ),
        check_vma=False,
    )
```

```python
import functools

import jax
import jax.numpy as jnp
from jax import lax
from jax.experimental import pallas as pl
from jax.experimental.pallas import tpu as pltpu
from jax.sharding import PartitionSpec as P

HEADS = 16
HEAD_DIM = 64
PARTS = 2


def moved(shard, to_blk=lambda b: b, to_rep=lambda r: r):
    n_blk, n_rep = lax.axis_size("blk"), lax.axis_size("rep")
    pairs = [
        (b * n_rep + r, to_blk(b) % n_blk * n_rep + to_rep(r))
        for b in range(n_blk)
        for r in range(n_rep)
    ]
    return lax.ppermute(shard, ("blk", "rep"), pairs)


def to_core(shard):
    return moved(shard, to_rep=lambda r: r ^ 1)


def to_partner(shard):
    return moved(shard, to_rep=lambda r: r ^ 2)


def to_cross(shard):
    return moved(shard, to_blk=lambda b: b ^ 1, to_rep=lambda r: r ^ 2)


def to_flip(shard):
    return moved(shard, to_blk=lambda b: b ^ 1)


def to_outer(shard):
    return moved(shard, to_blk=lambda b: b + 2 if b % 2 == 0 else b - 2)


def to_inner(shard):
    return moved(shard, to_blk=lambda b: b - 2 if b % 2 == 0 else b + 2)


def after(value, *earlier):
    return lax.optimization_barrier((value, *earlier))[0]


NT = (((1,), (1,)), ((), ()))
NN = (((1,), (0,)), ((), ()))
TN = (((0,), (0,)), ((), ()))


def mm(a, b, dims=NN):
    return lax.dot_general(a, b, dims, preferred_element_type=jnp.float32)


def project_kernel(jobs, n_x, n_w, *refs):
    xs, ws, outs = refs[:n_x], refs[n_x : n_x + n_w], refs[n_x + n_w :]
    for (x, w, dims), out in zip(jobs, outs):
        out[...] = mm(xs[x][...], ws[w][...], dims).astype(out.dtype)


def project(xs, ws, jobs, vmem_mib=63):
    rows, depth = xs[0].shape
    wide = 256
    steps = depth // wide
    whole = pl.BlockSpec((rows, depth), lambda i: (0, 0))
    transposed = {w: dims == NT for _, w, dims in jobs}
    return pl.pallas_call(
        functools.partial(project_kernel, jobs, len(xs), len(ws)),
        grid=(steps,),
        in_specs=[whole] * len(xs)
        + [
            pl.BlockSpec((wide, depth), lambda i: (i, 0))
            if transposed[w]
            else pl.BlockSpec((depth, wide), lambda i: (0, i))
            for w in range(len(ws))
        ],
        out_specs=[pl.BlockSpec((rows, wide), lambda i: (0, i))] * len(jobs),
        out_shape=[jax.ShapeDtypeStruct((rows, depth), jnp.bfloat16)] * len(jobs),
        compiler_params=pltpu.CompilerParams(vmem_limit_bytes=vmem_mib * 2**20),
        cost_estimate=pl.CostEstimate(
            flops=3 * len(jobs) * rows * depth * depth,
            bytes_accessed=2 * depth * (len(xs) * rows + len(ws) * depth + len(jobs) * rows),
            transcendentals=0,
        ),
        name="project",
    )(*xs, *ws)


def transpose_kernel(which, *refs):
    rows = refs[0].shape[0]
    for i, piece in enumerate(refs[:-1]):
        refs[-1][:, i * rows : (i + 1) * rows] = piece[...].T


def transposed_columns(which, pieces, wide):
    rows = pieces[0].shape[0]
    blocks = which.shape[0]
    return pl.pallas_call(
        transpose_kernel,
        grid_spec=pltpu.PrefetchScalarGridSpec(
            num_scalar_prefetch=1,
            grid=(blocks,),
            in_specs=[pl.BlockSpec((rows, wide), lambda i, which: (0, which[i]))] * len(pieces),
            out_specs=pl.BlockSpec((wide, rows * len(pieces)), lambda i, which: (i, 0)),
        ),
        out_shape=jax.ShapeDtypeStruct((blocks * wide, rows * len(pieces)), jnp.bfloat16),
        compiler_params=pltpu.CompilerParams(vmem_limit_bytes=63 * 2**20),
        cost_estimate=pl.CostEstimate(
            flops=10**9, bytes_accessed=4 * blocks * wide * rows * len(pieces), transcendentals=0
        ),
        name="transposed_columns",
    )(which, *pieces)


def weight_grad_kernel(n_set, n_step, x_cols, *refs):
    sets, (mine, theirs) = refs[:-2], refs[-2:]
    size = len(sets) // n_set
    half = mine.shape[0]
    step = pl.program_id(0)
    for which in range(n_set):

        @pl.when((step >= which * n_step) & (step < (which + 1) * n_step))
        def _():
            total = jnp.zeros((2 * half, mine.shape[1]), jnp.float32)
            at = 0
            for piece in sets[which * size : (which + 1) * size]:
                rows = piece.shape[0]
                total = total + mm(x_cols[:, at : at + rows], piece[...])
                at += rows
            mine[...] = total[:half]
            theirs[...] = total[half:].astype(theirs.dtype)


def weight_grads(x_cols, *sets):
    width = sets[0][0].shape[1]
    wide = 256
    n_step = width // wide
    half, depth = x_cols.shape[0] // 2, x_cols.shape[1]

    def columns(which):
        return lambda i: (0, jnp.clip(i - which * n_step, 0, n_step - 1))

    return pl.pallas_call(
        functools.partial(weight_grad_kernel, len(sets), n_step),
        grid=(len(sets) * n_step,),
        in_specs=[pl.BlockSpec((2 * half, depth), lambda i: (0, 0))]
        + [
            pl.BlockSpec((piece.shape[0], wide), columns(which))
            for which, pieces in enumerate(sets)
            for piece in pieces
        ],
        out_specs=[pl.BlockSpec((half, wide), lambda i: (0, i))] * 2,
        out_shape=[
            jax.ShapeDtypeStruct((half, len(sets) * width), jnp.float32),
            jax.ShapeDtypeStruct((half, len(sets) * width), jnp.bfloat16),
        ],
        compiler_params=pltpu.CompilerParams(vmem_limit_bytes=16 * 2**20),
        cost_estimate=pl.CostEstimate(
            flops=100 * half * depth * width * len(sets),
            bytes_accessed=2 * depth * (2 * half + width) + 6 * half * width,
            transcendentals=0,
        ),
        name="weight_grads",
    )(x_cols, *(piece for pieces in sets for piece in pieces))


def edge_kernel(n_row, n_band, width, col, slots, count, scale, mask, own_scale, *refs):
    ins, refs = refs[: 2 * n_row + 2 * n_band], refs[2 * n_row + 2 * n_band :]
    q_in, g_in = ins[:n_row], ins[n_row : 2 * n_row]
    k_in, v_in = ins[2 * n_row : 2 * n_row + n_band], ins[2 * n_row + n_band :]
    out_near, out_far, out_own, out_flip, out_side, out_back, out_diag = refs[:7]
    q_all, g_all, k_all, v_all, q_acc, k_acc, v_acc, sems = refs[7:]
    own_rows = k_in[0].shape[0]
    tile = mask.shape[-1]
    cols = pl.ds(col, width)
    copies = []
    for pieces, target in ((q_in, q_all), (g_in, g_all), (k_in, k_all), (v_in, v_all)):
        for at, piece in enumerate(pieces):
            copies.append(
                pltpu.make_async_copy(
                    piece.at[:, cols],
                    target.at[pl.ds(at * own_rows, own_rows), :],
                    sems.at[len(copies)],
                )
            )
    for copy in copies:
        copy.start()
    for acc in (q_acc, k_acc, v_acc):
        acc[own_rows:, :] = jnp.zeros((acc.shape[0] - own_rows, width), jnp.float32)
    for copy in copies:
        copy.wait()

    low = lax.broadcasted_iota(jnp.int32, (tile, tile), 1) < HEAD_DIM
    same_head = (lax.broadcasted_iota(jnp.int32, (tile, tile), 0) < HEAD_DIM) == low
    ones = same_head.astype(jnp.float32).astype(jnp.bfloat16)

    def split(part):
        zero = jnp.zeros_like(part)
        return jnp.concatenate([jnp.where(low, part, zero), jnp.where(low, zero, part)], axis=0)

    def head_sums(a, b):
        product = a * b
        head = product.astype(jnp.bfloat16)
        tail = (product - head.astype(jnp.float32)).astype(jnp.bfloat16)
        return mm(head, ones) + mm(tail, ones)

    for pair in range(width // tile):
        here = slice(pair * tile, (pair + 1) * tile)
        q, g, k, v = (
            ref[:own_rows, here].astype(jnp.float32) for ref in (q_all, g_all, k_all, v_all)
        )
        gate = jax.nn.sigmoid(head_sums(q, k) * HEAD_DIM**-0.5)
        weight = own_scale[...] * gate
        edge = weight * (1.0 - gate) * head_sums(g, v) * HEAD_DIM**-0.5
        q_acc[:own_rows, here] = edge * k
        k_acc[:own_rows, here] = edge * q
        v_acc[:own_rows, here] = weight * g

    def slot_step(slot, _):
        row_tile = slots[0, slot]
        rows = pl.ds(pl.multiple_of(row_tile * tile, tile), tile)
        band = pl.ds(pl.multiple_of(slots[1, slot] * tile, tile), tile)
        edge = mask[slot].astype(jnp.float32).T * scale[pl.ds(row_tile, 1), :]
        edge = jnp.concatenate([edge, edge], axis=1)
        pairs = [slice(p * tile, (p + 1) * tile) for p in range(width // tile)]
        for at in range(0, len(pairs), 4):
            todo = pairs[at : at + 4]
            scores = []
            for here in todo:
                keys, values = k_all[band, here], v_all[band, here]
                queries, grads = split(q_all[rows, here]), split(g_all[rows, here])
                scores.append((mm(keys, queries, NT), mm(values, grads, NT)))
            terms = []
            for score, agree in scores:
                gate = 0.5 * jnp.tanh(score * (0.5 * HEAD_DIM**-0.5)) + 0.5
                weight = edge * gate
                prob = weight.astype(jnp.bfloat16)
                grad = (weight * (1.0 - gate) * (agree * HEAD_DIM**-0.5)).astype(jnp.bfloat16)
                terms.append((prob, grad))
            for here, (prob, grad) in zip(todo, terms):
                queries, grads = split(q_all[rows, here]), split(g_all[rows, here])
                k_acc[band, here] += mm(grad, queries)
                v_acc[band, here] += mm(prob, grads)
                flat = jnp.concatenate([grad[:, :tile].T, grad[:, tile:].T], axis=1)
                q_acc[rows, here] += mm(flat, split(k_all[band, here]))
        return 0

    lax.fori_loop(0, count[0], slot_step, 0)
    near = out_near.shape[0]
    out_near[...] = q_acc[:near, :]
    out_far[...] = q_acc[near:, :].astype(jnp.bfloat16)
    for i, out in enumerate((out_own, out_side, out_back, out_flip, out_diag)):
        here = slice(i * own_rows, (i + 1) * own_rows)
        out[:, :width] = k_acc[here, :].astype(out.dtype)
        out[:, width:] = v_acc[here, :].astype(out.dtype)


def edge_pass(slots, count, scale, mask, own_scale, q, g, k, v, col, width):
    n_row, n_band, own_rows = len(q), len(k), k[0].shape[0]
    q_rows, band_rows = n_row * own_rows, n_band * own_rows
    vmem = pl.BlockSpec(memory_space=pltpu.VMEM)
    smem = pl.BlockSpec(memory_space=pltpu.SMEM)
    anywhere = pl.BlockSpec(memory_space=pl.ANY)
    pieces = (*q, *g, *k, *v)
    term = jax.ShapeDtypeStruct((own_rows, 2 * width), jnp.bfloat16)
    term_wide = jax.ShapeDtypeStruct((own_rows, 2 * width), jnp.float32)
    return pl.pallas_call(
        functools.partial(edge_kernel, n_row, n_band, width, col),
        out_shape=[
            jax.ShapeDtypeStruct((q_rows // 2, width), jnp.float32),
            jax.ShapeDtypeStruct((q_rows // 2, width), jnp.bfloat16),
            term_wide,
            term_wide,
            term,
            term,
            term,
        ],
        in_specs=[smem, smem, vmem, vmem, vmem] + [anywhere] * len(pieces),
        out_specs=[vmem] * 7,
        scratch_shapes=[
            pltpu.VMEM((q_rows, width), jnp.bfloat16),
            pltpu.VMEM((q_rows, width), jnp.bfloat16),
            pltpu.VMEM((band_rows, width), jnp.bfloat16),
            pltpu.VMEM((band_rows, width), jnp.bfloat16),
            pltpu.VMEM((q_rows, width), jnp.float32),
            pltpu.VMEM((band_rows, width), jnp.float32),
            pltpu.VMEM((band_rows, width), jnp.float32),
            pltpu.SemaphoreType.DMA((len(pieces),)),
        ],
        compiler_params=pltpu.CompilerParams(vmem_limit_bytes=48 * 2**20),
        cost_estimate=pl.CostEstimate(
            flops=mask.size * width, bytes_accessed=band_rows * width, transcendentals=0
        ),
        name="edges",
    )(slots, count, scale, mask, own_scale, *pieces)


def on_device(
    node_input,
    output_grad,
    saved_output,
    weight_query,
    weight_key,
    weight_value,
    weight_out,
    tile_slots,
    tile_mask,
    tile_count,
):
    bf16, f32 = jnp.bfloat16, jnp.float32
    own_rows, model_width = node_input.shape
    rep = lax.axis_index("rep")
    blk = lax.axis_index("blk")
    masks = tile_mask[0]
    n_slot, tile = masks.shape[0], masks.shape[-1]
    per_group = own_rows // tile
    n_rep = lax.axis_size("rep")

    group = tile_slots[0, 0] // per_group ^ rep
    place = (group >> 1) | ((group & 1) << 1)
    row_tile = place * per_group + tile_slots[0, 0] % per_group
    band = tile_slots[0, 1] // per_group
    offset = jnp.where(blk % 2 == 0, band - 2, 2 - band)
    band_place = jnp.where(
        offset == 0,
        0,
        jnp.where(offset == -2, 1, jnp.where(offset == 2, 2, jnp.where(offset == 1, 3, 4))),
    )
    slots = jnp.stack([row_tile, band_place * per_group + tile_slots[0, 1] % per_group])

    x_partner = to_partner(node_input)
    x_side = to_outer(node_input)
    x_back = to_inner(node_input)

    live = (jnp.arange(n_slot, dtype=jnp.int32) < tile_count[0]).astype(jnp.int32)
    row_sums = jnp.sum(masks, axis=2, dtype=jnp.int32) * live[:, None]
    picked = (
        row_tile[:, None] == jnp.arange(n_rep * per_group, dtype=jnp.int32)[None, :]
    ).astype(jnp.int32)
    degree = jnp.sum(picked[:, :, None] * row_sums[:, None, :], axis=0, dtype=jnp.int32)
    other = to_core(degree).reshape(2, 2 * per_group, tile)
    degree = degree + other[::-1].reshape(degree.shape)
    first = project(
        [node_input, output_grad],
        [weight_query, weight_out, weight_key, weight_value],
        [(0, 0, NN), (1, 1, NT), (0, 2, NN), (0, 3, NN)],
    )
    x_partner = after(x_partner, first[0])
    x_flip = to_cross(x_partner)
    x_cores = to_core(after(node_input, x_partner)), to_core(x_partner)
    y_partner = to_partner(after(output_grad, x_partner))
    x_rows = [node_input, x_partner, *x_cores]
    quarter = model_width // n_rep
    x_cols = transposed_columns(jnp.stack([rep, rep ^ 2]), x_rows, quarter)
    k_near = project(
        [after(x_side, x_cols), x_back],
        [weight_key, weight_value],
        [(x, w, NN) for w in range(2) for x in range(2)],
    )
    x_diag = to_outer(after(x_flip, k_near[0]))
    other = to_partner(after(degree, y_partner)).reshape(2, 2, per_group, tile)
    degree = degree + other[:, ::-1].reshape(degree.shape)
    scale = lax.rsqrt(1.0 + degree.astype(f32))
    own_scale = scale[:per_group].reshape(own_rows, 1)
    y_cores = to_core(after(output_grad, y_partner, k_near[0])), to_core(after(y_partner, k_near[0]))
    y_rows = [output_grad, y_partner, *y_cores]
    middle = project(
        [*x_rows[1:], x_flip, *y_rows[1:]],
        [weight_query, weight_out, weight_key, weight_value],
        [(x, 0, NN) for x in range(3)] + [(x, 1, NT) for x in range(4, 7)]
        + [(3, 2, NN), (3, 3, NN)],
    )
    queries, grads = [first[0], *middle[:3]], [first[1], *middle[3:6]]

    def quarter_of(array, which):
        return lax.dynamic_slice_in_dim(array, which * quarter, quarter, 1)

    core, chip = rep % 2, rep // 2
    s_partner = to_partner(
        lax.dynamic_slice_in_dim(
            after(saved_output, y_cores[1]), (1 - chip) * 2 * quarter, 2 * quarter, 1
        )
    )
    s_cols = [
        quarter_of(saved_output, rep),
        quarter_of(s_partner, core),
        to_core(quarter_of(after(saved_output, s_partner), rep ^ 1)),
        to_core(quarter_of(s_partner, 1 - core)),
    ]
    def weight_grad(sources, gradients):
        total = mm(sources[0], gradients[0], TN)
        for source, gradient in zip(sources[1:], gradients[1:]):
            total = total + mm(source, gradient, TN)
        return total

    def summed(*sets):
        mine, theirs = weight_grads(x_cols, *sets)
        return (mine + to_partner(theirs).astype(f32)).astype(bf16), theirs

    out_weight_grad = weight_grad(s_cols, after(y_rows, k_near[0])).astype(bf16)
    k_far = project(
        [after(x_diag, *s_cols[2:])], [weight_key, weight_value], [(0, 0, NN), (0, 1, NN)], 36
    )
    keys = [first[2], *k_near[:2], middle[6], k_far[0]]
    values = [first[3], *k_near[2:], middle[7], k_far[1]]

    width = model_width // PARTS

    def edges(part, *gate):
        return edge_pass(
            after(slots, *gate), tile_count, scale, masks, own_scale, queries, grads, keys,
            values, part * width, width,
        )

    def chip_terms(near, far):
        near = (near + to_core(far).astype(f32)).astype(bf16)
        return near, to_core(near)

    def crossed(flip, inner):
        return to_cross((flip + inner.astype(f32)).astype(bf16))

    def finish(part, totals, near, own, side, back, foreign):
        cols = slice(part * width, (part + 1) * width)
        w_query = weight_query[:, cols]
        w_key, w_value = weight_key[:, cols], weight_value[:, cols]
        kv = (own + side.astype(f32) + back.astype(f32)).astype(bf16)
        both = jnp.concatenate([kv, foreign], axis=0)
        totals = [
            total
            + mm(q, w_query, NT)
            + mm(terms[:, :width], w_key, NT)
            + mm(terms[:, width:], w_value, NT)
            for total, q, terms in (
                (totals[0], near[:own_rows], kv),
                (totals[1], near[own_rows:], foreign),
            )
        ]
        return totals, *summed([both, to_core(both)])

    near_0, far_0, own_0, flip_0, side_0, back_0, diag_0 = edges(0)
    q_0 = chip_terms(near_0, far_0)
    inner_0, side_0, back_0 = to_inner(diag_0), to_inner(side_0), to_outer(back_0)
    near_1, far_1, own_1, flip_1, side_1, back_1, diag_1 = edges(1, q_0[0], out_weight_grad)
    q_1 = chip_terms(near_1, far_1)
    own_0, flip_0 = after((own_0, flip_0), far_1)
    cross_0 = crossed(flip_0, inner_0)
    inner_1 = to_inner(after(diag_1, inner_0))
    query_grad, q_sent = summed(q_0, q_1)
    cross_1 = crossed(after(flip_1, q_sent), inner_1)
    totals, kv_grad_0, kv_sent = finish(
        0, (0.0, 0.0), q_0[0], own_0, side_0, back_0, after(cross_0, q_sent, query_grad)
    )
    side_1, back_1 = after((side_1, back_1), inner_1, q_sent)
    side_1, back_1 = after((to_inner(side_1), to_outer(back_1)), kv_sent)
    totals, kv_grad_1, _ = finish(
        1, totals, q_1[0], own_1, side_1, back_1, after(cross_1, kv_sent)
    )
    grad_partner = to_partner(after(totals[1], kv_grad_0).astype(bf16))
    input_grad = totals[0] + grad_partner.astype(f32)
    key_grads = [grad[:, :width] for grad in (kv_grad_0, kv_grad_1)]
    value_grads = [grad[:, width:] for grad in (kv_grad_0, kv_grad_1)]

    def joined(pieces):
        return jnp.concatenate(pieces, axis=1)[None]

    return (
        input_grad.astype(bf16),
        query_grad[None],
        joined(key_grads),
        joined(value_grads),
        out_weight_grad[None],
    )


def solution(mesh):
    placed = (
        P(("blk", "rep"), None),
        P(("blk", "rep"), None),
        P(("blk", "rep"), None),
        P(),
        P(),
        P(),
        P(),
        P(("blk", "rep"), None, None),
        P(("blk", "rep"), None, None, None),
        P(("blk", "rep")),
    )
    return jax.shard_map(
        on_device,
        mesh=mesh,
        in_specs=placed,
        out_specs=(
            P(("blk", "rep"), None),
            P("blk", "rep", None),
            P("blk", "rep", None),
            P("blk", "rep", None),
            P("blk", "rep", None),
        ),
        check_vma=False,
    )
```

```python
import functools

import jax
import jax.numpy as jnp
from jax import lax
from jax.experimental import pallas as pl
from jax.experimental.pallas import tpu as pltpu
from jax.sharding import PartitionSpec as P

HEADS = 16
HEAD_DIM = 64
PARTS = 2


def moved(shard, to_blk=lambda b: b, to_rep=lambda r: r):
    n_blk, n_rep = lax.axis_size("blk"), lax.axis_size("rep")
    pairs = [
        (b * n_rep + r, to_blk(b) % n_blk * n_rep + to_rep(r))
        for b in range(n_blk)
        for r in range(n_rep)
    ]
    return lax.ppermute(shard, ("blk", "rep"), pairs)


def to_core(shard):
    return moved(shard, to_rep=lambda r: r ^ 1)


def to_partner(shard):
    return moved(shard, to_rep=lambda r: r ^ 2)


def to_cross(shard):
    return moved(shard, to_blk=lambda b: b ^ 1, to_rep=lambda r: r ^ 2)


def to_flip(shard):
    return moved(shard, to_blk=lambda b: b ^ 1)


def to_outer(shard):
    return moved(shard, to_blk=lambda b: b + 2 if b % 2 == 0 else b - 2)


def to_inner(shard):
    return moved(shard, to_blk=lambda b: b - 2 if b % 2 == 0 else b + 2)


def after(value, *earlier):
    return lax.optimization_barrier((value, *earlier))[0]


NT = (((1,), (1,)), ((), ()))
NN = (((1,), (0,)), ((), ()))
TN = (((0,), (0,)), ((), ()))


def mm(a, b, dims=NN):
    return lax.dot_general(a, b, dims, preferred_element_type=jnp.float32)


def project_kernel(jobs, n_x, n_w, *refs):
    xs, ws, outs = refs[:n_x], refs[n_x : n_x + n_w], refs[n_x + n_w :]
    for (x, w, dims), out in zip(jobs, outs):
        out[...] = mm(xs[x][...], ws[w][...], dims).astype(out.dtype)


def project(xs, ws, jobs, vmem_mib=63):
    rows, depth = xs[0].shape
    wide = 256
    steps = depth // wide
    whole = pl.BlockSpec((rows, depth), lambda i: (0, 0))
    transposed = {w: dims == NT for _, w, dims in jobs}
    return pl.pallas_call(
        functools.partial(project_kernel, jobs, len(xs), len(ws)),
        grid=(steps,),
        in_specs=[whole] * len(xs)
        + [
            pl.BlockSpec((wide, depth), lambda i: (i, 0))
            if transposed[w]
            else pl.BlockSpec((depth, wide), lambda i: (0, i))
            for w in range(len(ws))
        ],
        out_specs=[pl.BlockSpec((rows, wide), lambda i: (0, i))] * len(jobs),
        out_shape=[jax.ShapeDtypeStruct((rows, depth), jnp.bfloat16)] * len(jobs),
        compiler_params=pltpu.CompilerParams(vmem_limit_bytes=vmem_mib * 2**20),
        cost_estimate=pl.CostEstimate(
            flops=3 * len(jobs) * rows * depth * depth,
            bytes_accessed=2 * depth * (len(xs) * rows + len(ws) * depth + len(jobs) * rows),
            transcendentals=0,
        ),
        name="project",
    )(*xs, *ws)


def transpose_kernel(which, *refs):
    rows = refs[0].shape[0]
    for i, piece in enumerate(refs[:-1]):
        refs[-1][:, i * rows : (i + 1) * rows] = piece[...].T


def transposed_columns(which, pieces, wide):
    rows = pieces[0].shape[0]
    blocks = which.shape[0]
    return pl.pallas_call(
        transpose_kernel,
        grid_spec=pltpu.PrefetchScalarGridSpec(
            num_scalar_prefetch=1,
            grid=(blocks,),
            in_specs=[pl.BlockSpec((rows, wide), lambda i, which: (0, which[i]))] * len(pieces),
            out_specs=pl.BlockSpec((wide, rows * len(pieces)), lambda i, which: (i, 0)),
        ),
        out_shape=jax.ShapeDtypeStruct((blocks * wide, rows * len(pieces)), jnp.bfloat16),
        compiler_params=pltpu.CompilerParams(vmem_limit_bytes=63 * 2**20),
        cost_estimate=pl.CostEstimate(
            flops=10**9, bytes_accessed=4 * blocks * wide * rows * len(pieces), transcendentals=0
        ),
        name="transposed_columns",
    )(which, *pieces)


def weight_grad_kernel(n_set, n_step, x_cols, *refs):
    sets, (mine, theirs) = refs[:-2], refs[-2:]
    size = len(sets) // n_set
    half = mine.shape[0]
    step = pl.program_id(0)
    for which in range(n_set):

        @pl.when((step >= which * n_step) & (step < (which + 1) * n_step))
        def _():
            total = jnp.zeros((2 * half, mine.shape[1]), jnp.float32)
            at = 0
            for piece in sets[which * size : (which + 1) * size]:
                rows = piece.shape[0]
                total = total + mm(x_cols[:, at : at + rows], piece[...])
                at += rows
            mine[...] = total[:half]
            theirs[...] = total[half:].astype(theirs.dtype)


def weight_grads(x_cols, *sets):
    width = sets[0][0].shape[1]
    wide = 256
    n_step = width // wide
    half, depth = x_cols.shape[0] // 2, x_cols.shape[1]

    def columns(which):
        return lambda i: (0, jnp.clip(i - which * n_step, 0, n_step - 1))

    return pl.pallas_call(
        functools.partial(weight_grad_kernel, len(sets), n_step),
        grid=(len(sets) * n_step,),
        in_specs=[pl.BlockSpec((2 * half, depth), lambda i: (0, 0))]
        + [
            pl.BlockSpec((piece.shape[0], wide), columns(which))
            for which, pieces in enumerate(sets)
            for piece in pieces
        ],
        out_specs=[pl.BlockSpec((half, wide), lambda i: (0, i))] * 2,
        out_shape=[
            jax.ShapeDtypeStruct((half, len(sets) * width), jnp.float32),
            jax.ShapeDtypeStruct((half, len(sets) * width), jnp.bfloat16),
        ],
        compiler_params=pltpu.CompilerParams(vmem_limit_bytes=16 * 2**20),
        cost_estimate=pl.CostEstimate(
            flops=100 * half * depth * width * len(sets),
            bytes_accessed=2 * depth * (2 * half + width) + 6 * half * width,
            transcendentals=0,
        ),
        name="weight_grads",
    )(x_cols, *(piece for pieces in sets for piece in pieces))


def edge_kernel(n_row, n_band, width, col, slots, count, scale, mask, own_scale, *refs):
    ins, refs = refs[: 2 * n_row + 2 * n_band], refs[2 * n_row + 2 * n_band :]
    q_in, g_in = ins[:n_row], ins[n_row : 2 * n_row]
    k_in, v_in = ins[2 * n_row : 2 * n_row + n_band], ins[2 * n_row + n_band :]
    out_near, out_far, out_own, out_flip, out_side, out_back, out_diag = refs[:7]
    q_all, g_all, k_all, v_all, q_acc, k_acc, v_acc, sems = refs[7:]
    own_rows = k_in[0].shape[0]
    tile = mask.shape[-1]
    cols = pl.ds(col, width)
    copies = []
    for pieces, target in ((q_in, q_all), (g_in, g_all), (k_in, k_all), (v_in, v_all)):
        for at, piece in enumerate(pieces):
            copies.append(
                pltpu.make_async_copy(
                    piece.at[:, cols],
                    target.at[pl.ds(at * own_rows, own_rows), :],
                    sems.at[len(copies)],
                )
            )
    for copy in copies:
        copy.start()
    for acc in (q_acc, k_acc, v_acc):
        acc[own_rows:, :] = jnp.zeros((acc.shape[0] - own_rows, width), jnp.float32)
    for copy in copies:
        copy.wait()

    low = lax.broadcasted_iota(jnp.int32, (tile, tile), 1) < HEAD_DIM
    same_head = (lax.broadcasted_iota(jnp.int32, (tile, tile), 0) < HEAD_DIM) == low
    ones = same_head.astype(jnp.float32).astype(jnp.bfloat16)

    def split(part):
        zero = jnp.zeros_like(part)
        return jnp.concatenate([jnp.where(low, part, zero), jnp.where(low, zero, part)], axis=0)

    def head_sums(a, b):
        product = a * b
        head = product.astype(jnp.bfloat16)
        tail = (product - head.astype(jnp.float32)).astype(jnp.bfloat16)
        return mm(head, ones) + mm(tail, ones)

    for pair in range(width // tile):
        here = slice(pair * tile, (pair + 1) * tile)
        q, g, k, v = (
            ref[:own_rows, here].astype(jnp.float32) for ref in (q_all, g_all, k_all, v_all)
        )
        gate = jax.nn.sigmoid(head_sums(q, k) * HEAD_DIM**-0.5)
        weight = own_scale[...] * gate
        edge = weight * (1.0 - gate) * head_sums(g, v) * HEAD_DIM**-0.5
        q_acc[:own_rows, here] = edge * k
        k_acc[:own_rows, here] = edge * q
        v_acc[:own_rows, here] = weight * g

    def slot_step(slot, _):
        row_tile = slots[0, slot]
        rows = pl.ds(pl.multiple_of(row_tile * tile, tile), tile)
        band = pl.ds(pl.multiple_of(slots[1, slot] * tile, tile), tile)
        edge = mask[slot].astype(jnp.float32).T * scale[pl.ds(row_tile, 1), :]
        edge = jnp.concatenate([edge, edge], axis=1)
        pairs = [slice(p * tile, (p + 1) * tile) for p in range(width // tile)]
        for at in range(0, len(pairs), 4):
            todo = pairs[at : at + 4]
            scores = []
            for here in todo:
                keys, values = k_all[band, here], v_all[band, here]
                queries, grads = split(q_all[rows, here]), split(g_all[rows, here])
                scores.append((mm(keys, queries, NT), mm(values, grads, NT)))
            terms = []
            for score, agree in scores:
                gate = 0.5 * jnp.tanh(score * (0.5 * HEAD_DIM**-0.5)) + 0.5
                weight = edge * gate
                prob = weight.astype(jnp.bfloat16)
                grad = (weight * (1.0 - gate) * (agree * HEAD_DIM**-0.5)).astype(jnp.bfloat16)
                terms.append((prob, grad))
            for here, (prob, grad) in zip(todo, terms):
                queries, grads = split(q_all[rows, here]), split(g_all[rows, here])
                k_acc[band, here] += mm(grad, queries)
                v_acc[band, here] += mm(prob, grads)
                flat = jnp.concatenate([grad[:, :tile].T, grad[:, tile:].T], axis=1)
                q_acc[rows, here] += mm(flat, split(k_all[band, here]))
        return 0

    lax.fori_loop(0, count[0], slot_step, 0)
    near = out_near.shape[0]
    out_near[...] = q_acc[:near, :]
    out_far[...] = q_acc[near:, :].astype(jnp.bfloat16)
    for i, out in enumerate((out_own, out_side, out_back, out_flip, out_diag)):
        here = slice(i * own_rows, (i + 1) * own_rows)
        out[:, :width] = k_acc[here, :].astype(out.dtype)
        out[:, width:] = v_acc[here, :].astype(out.dtype)


def edge_pass(slots, count, scale, mask, own_scale, q, g, k, v, col, width):
    n_row, n_band, own_rows = len(q), len(k), k[0].shape[0]
    q_rows, band_rows = n_row * own_rows, n_band * own_rows
    vmem = pl.BlockSpec(memory_space=pltpu.VMEM)
    smem = pl.BlockSpec(memory_space=pltpu.SMEM)
    anywhere = pl.BlockSpec(memory_space=pl.ANY)
    pieces = (*q, *g, *k, *v)
    term = jax.ShapeDtypeStruct((own_rows, 2 * width), jnp.bfloat16)
    term_wide = jax.ShapeDtypeStruct((own_rows, 2 * width), jnp.float32)
    return pl.pallas_call(
        functools.partial(edge_kernel, n_row, n_band, width, col),
        out_shape=[
            jax.ShapeDtypeStruct((q_rows // 2, width), jnp.float32),
            jax.ShapeDtypeStruct((q_rows // 2, width), jnp.bfloat16),
            term_wide,
            term_wide,
            term,
            term,
            term,
        ],
        in_specs=[smem, smem, vmem, vmem, vmem] + [anywhere] * len(pieces),
        out_specs=[vmem] * 7,
        scratch_shapes=[
            pltpu.VMEM((q_rows, width), jnp.bfloat16),
            pltpu.VMEM((q_rows, width), jnp.bfloat16),
            pltpu.VMEM((band_rows, width), jnp.bfloat16),
            pltpu.VMEM((band_rows, width), jnp.bfloat16),
            pltpu.VMEM((q_rows, width), jnp.float32),
            pltpu.VMEM((band_rows, width), jnp.float32),
            pltpu.VMEM((band_rows, width), jnp.float32),
            pltpu.SemaphoreType.DMA((len(pieces),)),
        ],
        compiler_params=pltpu.CompilerParams(vmem_limit_bytes=48 * 2**20),
        cost_estimate=pl.CostEstimate(
            flops=mask.size * width, bytes_accessed=band_rows * width, transcendentals=0
        ),
        name="edges",
    )(slots, count, scale, mask, own_scale, *pieces)


def on_device(
    node_input,
    output_grad,
    saved_output,
    weight_query,
    weight_key,
    weight_value,
    weight_out,
    tile_slots,
    tile_mask,
    tile_count,
):
    bf16, f32 = jnp.bfloat16, jnp.float32
    own_rows, model_width = node_input.shape
    rep = lax.axis_index("rep")
    blk = lax.axis_index("blk")
    masks = tile_mask[0]
    n_slot, tile = masks.shape[0], masks.shape[-1]
    per_group = own_rows // tile
    n_rep = lax.axis_size("rep")

    group = tile_slots[0, 0] // per_group ^ rep
    place = (group >> 1) | ((group & 1) << 1)
    row_tile = place * per_group + tile_slots[0, 0] % per_group
    band = tile_slots[0, 1] // per_group
    offset = jnp.where(blk % 2 == 0, band - 2, 2 - band)
    band_place = jnp.where(
        offset == 0,
        0,
        jnp.where(offset == -2, 1, jnp.where(offset == 2, 2, jnp.where(offset == 1, 3, 4))),
    )
    slots = jnp.stack([row_tile, band_place * per_group + tile_slots[0, 1] % per_group])

    x_partner = to_partner(node_input)
    x_side = to_outer(node_input)
    x_back = to_inner(node_input)

    live = (jnp.arange(n_slot, dtype=jnp.int32) < tile_count[0]).astype(jnp.int32)
    row_sums = jnp.sum(masks, axis=2, dtype=jnp.int32) * live[:, None]
    picked = (
        row_tile[:, None] == jnp.arange(n_rep * per_group, dtype=jnp.int32)[None, :]
    ).astype(jnp.int32)
    degree = jnp.sum(picked[:, :, None] * row_sums[:, None, :], axis=0, dtype=jnp.int32)
    other = to_core(degree).reshape(2, 2 * per_group, tile)
    degree = degree + other[::-1].reshape(degree.shape)
    first = project(
        [node_input, output_grad],
        [weight_query, weight_out, weight_key, weight_value],
        [(0, 0, NN), (1, 1, NT), (0, 2, NN), (0, 3, NN)],
    )
    x_partner = after(x_partner, first[0])
    x_flip = to_cross(x_partner)
    x_cores = to_core(after(node_input, x_partner)), to_core(x_partner)
    y_partner = to_partner(after(output_grad, x_partner))
    x_rows = [node_input, x_partner, *x_cores]
    quarter = model_width // n_rep
    x_cols = transposed_columns(jnp.stack([rep, rep ^ 2]), x_rows, quarter)
    k_near = project(
        [after(x_side, x_cols), x_back],
        [weight_key, weight_value],
        [(x, w, NN) for w in range(2) for x in range(2)],
    )
    x_diag = to_outer(after(x_flip, k_near[0]))
    other = to_partner(after(degree, y_partner)).reshape(2, 2, per_group, tile)
    degree = degree + other[:, ::-1].reshape(degree.shape)
    scale = lax.rsqrt(1.0 + degree.astype(f32))
    own_scale = scale[:per_group].reshape(own_rows, 1)
    y_cores = to_core(after(output_grad, y_partner, k_near[0])), to_core(after(y_partner, k_near[0]))
    y_rows = [output_grad, y_partner, *y_cores]
    middle = project(
        [*x_rows[1:], x_flip, *y_rows[1:]],
        [weight_query, weight_out, weight_key, weight_value],
        [(x, 0, NN) for x in range(3)] + [(x, 1, NT) for x in range(4, 7)]
        + [(3, 2, NN), (3, 3, NN)],
    )
    queries, grads = [first[0], *middle[:3]], [first[1], *middle[3:6]]

    def quarter_of(array, which):
        return lax.dynamic_slice_in_dim(array, which * quarter, quarter, 1)

    core, chip = rep % 2, rep // 2
    s_partner = to_partner(
        lax.dynamic_slice_in_dim(
            after(saved_output, y_cores[1]), (1 - chip) * 2 * quarter, 2 * quarter, 1
        )
    )
    s_cols = [
        quarter_of(saved_output, rep),
        quarter_of(s_partner, core),
        to_core(quarter_of(after(saved_output, s_partner), rep ^ 1)),
        to_core(quarter_of(s_partner, 1 - core)),
    ]
    def weight_grad(sources, gradients):
        total = mm(sources[0], gradients[0], TN)
        for source, gradient in zip(sources[1:], gradients[1:]):
            total = total + mm(source, gradient, TN)
        return total

    def summed(*sets):
        mine, theirs = weight_grads(x_cols, *sets)
        return (mine + to_partner(theirs).astype(f32)).astype(bf16), theirs

    k_far = project(
        [after(x_diag, *s_cols[2:])], [weight_key, weight_value], [(0, 0, NN), (0, 1, NN)], 36
    )
    keys = [first[2], *k_near[:2], middle[6], k_far[0]]
    values = [first[3], *k_near[2:], middle[7], k_far[1]]

    width = model_width // PARTS

    def edges(part, *gate):
        return edge_pass(
            after(slots, *gate), tile_count, scale, masks, own_scale, queries, grads, keys,
            values, part * width, width,
        )

    def chip_terms(near, far):
        near = (near + to_core(far).astype(f32)).astype(bf16)
        return near, to_core(near)

    def crossed(flip, inner):
        return to_cross((flip + inner.astype(f32)).astype(bf16))

    def finish(part, totals, near, own, side, back, foreign):
        cols = slice(part * width, (part + 1) * width)
        w_query = weight_query[:, cols]
        w_key, w_value = weight_key[:, cols], weight_value[:, cols]
        kv = (own + side.astype(f32) + back.astype(f32)).astype(bf16)
        both = jnp.concatenate([kv, foreign], axis=0)
        totals = [
            total
            + mm(q, w_query, NT)
            + mm(terms[:, :width], w_key, NT)
            + mm(terms[:, width:], w_value, NT)
            for total, q, terms in (
                (totals[0], near[:own_rows], kv),
                (totals[1], near[own_rows:], foreign),
            )
        ]
        return totals, *summed([both, to_core(both)])

    near_0, far_0, own_0, flip_0, side_0, back_0, diag_0 = edges(0)
    q_0 = chip_terms(near_0, far_0)
    inner_0, back_0 = to_inner(diag_0), to_outer(back_0)
    side_0 = to_inner(after(side_0, q_0[0]))
    near_1, far_1, own_1, flip_1, side_1, back_1, diag_1 = edges(1, q_0[0])
    q_1 = chip_terms(near_1, far_1)
    flip_0 = after(flip_0, far_1)
    met_0 = (flip_0 + inner_0.astype(f32)).astype(bf16)
    cross_0 = to_cross(met_0)
    inner_1 = to_inner(after(diag_1, inner_0, q_0[1]))
    query_grad, q_sent = summed(q_0, q_1)
    side_0, back_0 = after((side_0, back_0), q_sent)
    out_weight_grad = weight_grad(s_cols, after(y_rows, met_0)).astype(bf16)
    cross_1 = crossed(after(flip_1, q_sent), inner_1)
    totals, kv_grad_0, kv_sent = finish(
        0, (0.0, 0.0), q_0[0], own_0, side_0, back_0, after(cross_0, q_sent, query_grad)
    )
    side_1, back_1 = after((side_1, back_1), inner_1, q_sent)
    side_1, back_1 = after((to_inner(side_1), to_outer(back_1)), kv_sent)
    totals, kv_grad_1, _ = finish(
        1, totals, q_1[0], own_1, side_1, back_1, after(cross_1, kv_sent)
    )
    grad_partner = to_partner(after(totals[1], kv_grad_0).astype(bf16))
    input_grad = totals[0] + grad_partner.astype(f32)
    key_grads = [grad[:, :width] for grad in (kv_grad_0, kv_grad_1)]
    value_grads = [grad[:, width:] for grad in (kv_grad_0, kv_grad_1)]

    def joined(pieces):
        return jnp.concatenate(pieces, axis=1)[None]

    return (
        input_grad.astype(bf16),
        query_grad[None],
        joined(key_grads),
        joined(value_grads),
        out_weight_grad[None],
    )


def solution(mesh):
    placed = (
        P(("blk", "rep"), None),
        P(("blk", "rep"), None),
        P(("blk", "rep"), None),
        P(),
        P(),
        P(),
        P(),
        P(("blk", "rep"), None, None),
        P(("blk", "rep"), None, None, None),
        P(("blk", "rep")),
    )
    return jax.shard_map(
        on_device,
        mesh=mesh,
        in_specs=placed,
        out_specs=(
            P(("blk", "rep"), None),
            P("blk", "rep", None),
            P("blk", "rep", None),
            P("blk", "rep", None),
            P("blk", "rep", None),
        ),
        check_vma=False,
    )
```

```python
import functools

import jax
import jax.numpy as jnp
from jax import lax
from jax.experimental import pallas as pl
from jax.experimental.pallas import tpu as pltpu
from jax.sharding import PartitionSpec as P

HEADS = 16
HEAD_DIM = 64
PARTS = 2


def moved(shard, to_blk=lambda b: b, to_rep=lambda r: r):
    n_blk, n_rep = lax.axis_size("blk"), lax.axis_size("rep")
    pairs = [
        (b * n_rep + r, to_blk(b) % n_blk * n_rep + to_rep(r))
        for b in range(n_blk)
        for r in range(n_rep)
    ]
    return lax.ppermute(shard, ("blk", "rep"), pairs)


def to_core(shard):
    return moved(shard, to_rep=lambda r: r ^ 1)


def to_partner(shard):
    return moved(shard, to_rep=lambda r: r ^ 2)


def to_cross(shard):
    return moved(shard, to_blk=lambda b: b ^ 1, to_rep=lambda r: r ^ 2)


def to_flip(shard):
    return moved(shard, to_blk=lambda b: b ^ 1)


def to_outer(shard):
    return moved(shard, to_blk=lambda b: b + 2 if b % 2 == 0 else b - 2)


def to_inner(shard):
    return moved(shard, to_blk=lambda b: b - 2 if b % 2 == 0 else b + 2)


def after(value, *earlier):
    return lax.optimization_barrier((value, *earlier))[0]


NT = (((1,), (1,)), ((), ()))
NN = (((1,), (0,)), ((), ()))
TN = (((0,), (0,)), ((), ()))


def mm(a, b, dims=NN):
    return lax.dot_general(a, b, dims, preferred_element_type=jnp.float32)


def project_kernel(jobs, n_x, n_w, *refs):
    xs, ws, outs = refs[:n_x], refs[n_x : n_x + n_w], refs[n_x + n_w :]
    for (x, w, dims), out in zip(jobs, outs):
        out[...] = mm(xs[x][...], ws[w][...], dims).astype(out.dtype)


def project(xs, ws, jobs, vmem_mib=63):
    rows, depth = xs[0].shape
    wide = 256
    steps = depth // wide
    whole = pl.BlockSpec((rows, depth), lambda i: (0, 0))
    transposed = {w: dims == NT for _, w, dims in jobs}
    return pl.pallas_call(
        functools.partial(project_kernel, jobs, len(xs), len(ws)),
        grid=(steps,),
        in_specs=[whole] * len(xs)
        + [
            pl.BlockSpec((wide, depth), lambda i: (i, 0))
            if transposed[w]
            else pl.BlockSpec((depth, wide), lambda i: (0, i))
            for w in range(len(ws))
        ],
        out_specs=[pl.BlockSpec((rows, wide), lambda i: (0, i))] * len(jobs),
        out_shape=[jax.ShapeDtypeStruct((rows, depth), jnp.bfloat16)] * len(jobs),
        compiler_params=pltpu.CompilerParams(vmem_limit_bytes=vmem_mib * 2**20),
        cost_estimate=pl.CostEstimate(
            flops=3 * len(jobs) * rows * depth * depth,
            bytes_accessed=2 * depth * (len(xs) * rows + len(ws) * depth + len(jobs) * rows),
            transcendentals=0,
        ),
        name="project",
    )(*xs, *ws)


def transpose_kernel(which, *refs):
    rows = refs[0].shape[0]
    for i, piece in enumerate(refs[:-1]):
        refs[-1][:, i * rows : (i + 1) * rows] = piece[...].T


def transposed_columns(which, pieces, wide):
    rows = pieces[0].shape[0]
    blocks = which.shape[0]
    return pl.pallas_call(
        transpose_kernel,
        grid_spec=pltpu.PrefetchScalarGridSpec(
            num_scalar_prefetch=1,
            grid=(blocks,),
            in_specs=[pl.BlockSpec((rows, wide), lambda i, which: (0, which[i]))] * len(pieces),
            out_specs=pl.BlockSpec((wide, rows * len(pieces)), lambda i, which: (i, 0)),
        ),
        out_shape=jax.ShapeDtypeStruct((blocks * wide, rows * len(pieces)), jnp.bfloat16),
        compiler_params=pltpu.CompilerParams(vmem_limit_bytes=63 * 2**20),
        cost_estimate=pl.CostEstimate(
            flops=10**9, bytes_accessed=4 * blocks * wide * rows * len(pieces), transcendentals=0
        ),
        name="transposed_columns",
    )(which, *pieces)


def weight_grad_kernel(n_set, n_step, x_cols, *refs):
    sets, (mine, theirs) = refs[:-2], refs[-2:]
    size = len(sets) // n_set
    half = mine.shape[0]
    step = pl.program_id(0)
    for which in range(n_set):

        @pl.when((step >= which * n_step) & (step < (which + 1) * n_step))
        def _():
            total = jnp.zeros((2 * half, mine.shape[1]), jnp.float32)
            at = 0
            for piece in sets[which * size : (which + 1) * size]:
                rows = piece.shape[0]
                total = total + mm(x_cols[:, at : at + rows], piece[...])
                at += rows
            mine[...] = total[:half]
            theirs[...] = total[half:].astype(theirs.dtype)


def weight_grads(x_cols, *sets):
    width = sets[0][0].shape[1]
    wide = 256
    n_step = width // wide
    half, depth = x_cols.shape[0] // 2, x_cols.shape[1]

    def columns(which):
        return lambda i: (0, jnp.clip(i - which * n_step, 0, n_step - 1))

    return pl.pallas_call(
        functools.partial(weight_grad_kernel, len(sets), n_step),
        grid=(len(sets) * n_step,),
        in_specs=[pl.BlockSpec((2 * half, depth), lambda i: (0, 0))]
        + [
            pl.BlockSpec((piece.shape[0], wide), columns(which))
            for which, pieces in enumerate(sets)
            for piece in pieces
        ],
        out_specs=[pl.BlockSpec((half, wide), lambda i: (0, i))] * 2,
        out_shape=[
            jax.ShapeDtypeStruct((half, len(sets) * width), jnp.float32),
            jax.ShapeDtypeStruct((half, len(sets) * width), jnp.bfloat16),
        ],
        compiler_params=pltpu.CompilerParams(vmem_limit_bytes=16 * 2**20),
        cost_estimate=pl.CostEstimate(
            flops=100 * half * depth * width * len(sets),
            bytes_accessed=2 * depth * (2 * half + width) + 6 * half * width,
            transcendentals=0,
        ),
        name="weight_grads",
    )(x_cols, *(piece for pieces in sets for piece in pieces))


def edge_kernel(n_row, n_band, width, col, slots, count, scale, mask, own_scale, *refs):
    ins, refs = refs[: 2 * n_row + 2 * n_band], refs[2 * n_row + 2 * n_band :]
    q_in, g_in = ins[:n_row], ins[n_row : 2 * n_row]
    k_in, v_in = ins[2 * n_row : 2 * n_row + n_band], ins[2 * n_row + n_band :]
    out_near, out_far, out_own, out_flip, out_side, out_back, out_diag = refs[:7]
    q_all, g_all, k_all, v_all, q_acc, k_acc, v_acc, sems = refs[7:]
    own_rows = k_in[0].shape[0]
    tile = mask.shape[-1]
    cols = pl.ds(col, width)
    copies = []
    for pieces, target in ((q_in, q_all), (g_in, g_all), (k_in, k_all), (v_in, v_all)):
        for at, piece in enumerate(pieces):
            copies.append(
                pltpu.make_async_copy(
                    piece.at[:, cols],
                    target.at[pl.ds(at * own_rows, own_rows), :],
                    sems.at[len(copies)],
                )
            )
    for copy in copies:
        copy.start()
    for acc in (q_acc, k_acc, v_acc):
        acc[own_rows:, :] = jnp.zeros((acc.shape[0] - own_rows, width), jnp.float32)
    for copy in copies:
        copy.wait()

    low = lax.broadcasted_iota(jnp.int32, (tile, tile), 1) < HEAD_DIM
    same_head = (lax.broadcasted_iota(jnp.int32, (tile, tile), 0) < HEAD_DIM) == low
    ones = same_head.astype(jnp.float32).astype(jnp.bfloat16)

    def split(part):
        zero = jnp.zeros_like(part)
        return jnp.concatenate([jnp.where(low, part, zero), jnp.where(low, zero, part)], axis=0)

    def head_sums(a, b):
        product = a * b
        head = product.astype(jnp.bfloat16)
        tail = (product - head.astype(jnp.float32)).astype(jnp.bfloat16)
        return mm(head, ones) + mm(tail, ones)

    for pair in range(width // tile):
        here = slice(pair * tile, (pair + 1) * tile)
        q, g, k, v = (
            ref[:own_rows, here].astype(jnp.float32) for ref in (q_all, g_all, k_all, v_all)
        )
        gate = jax.nn.sigmoid(head_sums(q, k) * HEAD_DIM**-0.5)
        weight = own_scale[...] * gate
        edge = weight * (1.0 - gate) * head_sums(g, v) * HEAD_DIM**-0.5
        q_acc[:own_rows, here] = edge * k
        k_acc[:own_rows, here] = edge * q
        v_acc[:own_rows, here] = weight * g

    def slot_step(slot, _):
        row_tile = slots[0, slot]
        rows = pl.ds(pl.multiple_of(row_tile * tile, tile), tile)
        band = pl.ds(pl.multiple_of(slots[1, slot] * tile, tile), tile)
        edge = mask[slot].astype(jnp.float32).T * scale[pl.ds(row_tile, 1), :]
        edge = jnp.concatenate([edge, edge], axis=1)
        pairs = [slice(p * tile, (p + 1) * tile) for p in range(width // tile)]
        for at in range(0, len(pairs), 4):
            todo = pairs[at : at + 4]
            scores = []
            for here in todo:
                keys, values = k_all[band, here], v_all[band, here]
                queries, grads = split(q_all[rows, here]), split(g_all[rows, here])
                scores.append((mm(keys, queries, NT), mm(values, grads, NT)))
            terms = []
            for score, agree in scores:
                gate = 0.5 * jnp.tanh(score * (0.5 * HEAD_DIM**-0.5)) + 0.5
                weight = edge * gate
                prob = weight.astype(jnp.bfloat16)
                grad = (weight * (1.0 - gate) * (agree * HEAD_DIM**-0.5)).astype(jnp.bfloat16)
                terms.append((prob, grad))
            for here, (prob, grad) in zip(todo, terms):
                queries, grads = split(q_all[rows, here]), split(g_all[rows, here])
                k_acc[band, here] += mm(grad, queries)
                v_acc[band, here] += mm(prob, grads)
                flat = jnp.concatenate([grad[:, :tile].T, grad[:, tile:].T], axis=1)
                q_acc[rows, here] += mm(flat, split(k_all[band, here]))
        return 0

    lax.fori_loop(0, count[0], slot_step, 0)
    near = out_near.shape[0]
    out_near[...] = q_acc[:near, :]
    out_far[...] = q_acc[near:, :].astype(jnp.bfloat16)
    for i, out in enumerate((out_own, out_side, out_back, out_flip, out_diag)):
        here = slice(i * own_rows, (i + 1) * own_rows)
        out[:, :width] = k_acc[here, :].astype(out.dtype)
        out[:, width:] = v_acc[here, :].astype(out.dtype)


def edge_pass(slots, count, scale, mask, own_scale, q, g, k, v, col, width):
    n_row, n_band, own_rows = len(q), len(k), k[0].shape[0]
    q_rows, band_rows = n_row * own_rows, n_band * own_rows
    vmem = pl.BlockSpec(memory_space=pltpu.VMEM)
    smem = pl.BlockSpec(memory_space=pltpu.SMEM)
    anywhere = pl.BlockSpec(memory_space=pl.ANY)
    pieces = (*q, *g, *k, *v)
    term = jax.ShapeDtypeStruct((own_rows, 2 * width), jnp.bfloat16)
    term_wide = jax.ShapeDtypeStruct((own_rows, 2 * width), jnp.float32)
    return pl.pallas_call(
        functools.partial(edge_kernel, n_row, n_band, width, col),
        out_shape=[
            jax.ShapeDtypeStruct((q_rows // 2, width), jnp.float32),
            jax.ShapeDtypeStruct((q_rows // 2, width), jnp.bfloat16),
            term_wide,
            term_wide,
            term,
            term,
            term,
        ],
        in_specs=[smem, smem, vmem, vmem, vmem] + [anywhere] * len(pieces),
        out_specs=[vmem] * 7,
        scratch_shapes=[
            pltpu.VMEM((q_rows, width), jnp.bfloat16),
            pltpu.VMEM((q_rows, width), jnp.bfloat16),
            pltpu.VMEM((band_rows, width), jnp.bfloat16),
            pltpu.VMEM((band_rows, width), jnp.bfloat16),
            pltpu.VMEM((q_rows, width), jnp.float32),
            pltpu.VMEM((band_rows, width), jnp.float32),
            pltpu.VMEM((band_rows, width), jnp.float32),
            pltpu.SemaphoreType.DMA((len(pieces),)),
        ],
        compiler_params=pltpu.CompilerParams(vmem_limit_bytes=48 * 2**20),
        cost_estimate=pl.CostEstimate(
            flops=mask.size * width, bytes_accessed=band_rows * width, transcendentals=0
        ),
        name="edges",
    )(slots, count, scale, mask, own_scale, *pieces)


def on_device(
    node_input,
    output_grad,
    saved_output,
    weight_query,
    weight_key,
    weight_value,
    weight_out,
    tile_slots,
    tile_mask,
    tile_count,
):
    bf16, f32 = jnp.bfloat16, jnp.float32
    own_rows, model_width = node_input.shape
    rep = lax.axis_index("rep")
    blk = lax.axis_index("blk")
    masks = tile_mask[0]
    n_slot, tile = masks.shape[0], masks.shape[-1]
    per_group = own_rows // tile
    n_rep = lax.axis_size("rep")

    group = tile_slots[0, 0] // per_group ^ rep
    place = (group >> 1) | ((group & 1) << 1)
    row_tile = place * per_group + tile_slots[0, 0] % per_group
    band = tile_slots[0, 1] // per_group
    offset = jnp.where(blk % 2 == 0, band - 2, 2 - band)
    band_place = jnp.where(
        offset == 0,
        0,
        jnp.where(offset == -2, 1, jnp.where(offset == 2, 2, jnp.where(offset == 1, 3, 4))),
    )
    slots = jnp.stack([row_tile, band_place * per_group + tile_slots[0, 1] % per_group])

    x_partner = to_partner(node_input)
    x_side = to_outer(node_input)
    x_back = to_inner(node_input)

    live = (jnp.arange(n_slot, dtype=jnp.int32) < tile_count[0]).astype(jnp.int32)
    row_sums = jnp.sum(masks, axis=2, dtype=jnp.int32) * live[:, None]
    picked = (
        row_tile[:, None] == jnp.arange(n_rep * per_group, dtype=jnp.int32)[None, :]
    ).astype(jnp.int32)
    degree = jnp.sum(picked[:, :, None] * row_sums[:, None, :], axis=0, dtype=jnp.int32)
    other = to_core(degree).reshape(2, 2 * per_group, tile)
    degree = degree + other[::-1].reshape(degree.shape)
    first = project(
        [node_input, output_grad],
        [weight_query, weight_out, weight_key, weight_value],
        [(0, 0, NN), (1, 1, NT), (0, 2, NN), (0, 3, NN)],
    )
    x_partner = after(x_partner, first[0])
    x_flip = to_cross(x_partner)
    x_cores = to_core(after(node_input, x_partner)), to_core(x_partner)
    y_partner = to_partner(after(output_grad, x_partner))
    x_rows = [node_input, x_partner, *x_cores]
    quarter = model_width // n_rep
    x_cols = transposed_columns(jnp.stack([rep, rep ^ 2]), x_rows, quarter)
    k_near = project(
        [after(x_side, x_cols), x_back],
        [weight_key, weight_value],
        [(x, w, NN) for w in range(2) for x in range(2)],
    )
    x_diag = to_outer(after(x_flip, k_near[0]))
    other = to_partner(after(degree, y_partner)).reshape(2, 2, per_group, tile)
    degree = degree + other[:, ::-1].reshape(degree.shape)
    scale = lax.rsqrt(1.0 + degree.astype(f32))
    own_scale = scale[:per_group].reshape(own_rows, 1)
    y_cores = to_core(after(output_grad, y_partner, k_near[0])), to_core(after(y_partner, k_near[0]))
    y_rows = [output_grad, y_partner, *y_cores]
    middle = project(
        [*x_rows[1:], x_flip, *y_rows[1:]],
        [weight_query, weight_out, weight_key, weight_value],
        [(x, 0, NN) for x in range(3)] + [(x, 1, NT) for x in range(4, 7)]
        + [(3, 2, NN), (3, 3, NN)],
    )
    queries, grads = [first[0], *middle[:3]], [first[1], *middle[3:6]]

    def quarter_of(array, which):
        return lax.dynamic_slice_in_dim(array, which * quarter, quarter, 1)

    core, chip = rep % 2, rep // 2
    s_partner = to_partner(
        lax.dynamic_slice_in_dim(
            after(saved_output, y_cores[1]), (1 - chip) * 2 * quarter, 2 * quarter, 1
        )
    )
    s_cols = [
        quarter_of(saved_output, rep),
        quarter_of(s_partner, core),
        to_core(quarter_of(after(saved_output, s_partner), rep ^ 1)),
        to_core(quarter_of(s_partner, 1 - core)),
    ]
    def weight_grad(sources, gradients):
        total = mm(sources[0], gradients[0], TN)
        for source, gradient in zip(sources[1:], gradients[1:]):
            total = total + mm(source, gradient, TN)
        return total

    def summed(*sets):
        mine, theirs = weight_grads(x_cols, *sets)
        return (mine + to_partner(theirs).astype(f32)).astype(bf16), theirs

    out_weight_grad = weight_grad(s_cols, after(y_rows, k_near[0])).astype(bf16)
    k_far = project(
        [after(x_diag, *s_cols[2:])], [weight_key, weight_value], [(0, 0, NN), (0, 1, NN)], 36
    )
    keys = [first[2], *k_near[:2], middle[6], k_far[0]]
    values = [first[3], *k_near[2:], middle[7], k_far[1]]

    width = model_width // PARTS

    def edges(part, *gate):
        return edge_pass(
            after(slots, *gate), tile_count, scale, masks, own_scale, queries, grads, keys,
            values, part * width, width,
        )

    def chip_terms(near, far):
        near = (near + to_core(far).astype(f32)).astype(bf16)
        return near, to_core(near)

    def crossed(flip, inner):
        return to_cross((flip + inner.astype(f32)).astype(bf16))

    def finish(part, totals, near, own, side, back, foreign):
        cols = slice(part * width, (part + 1) * width)
        w_query = weight_query[:, cols]
        w_key, w_value = weight_key[:, cols], weight_value[:, cols]
        kv = (own + side.astype(f32) + back.astype(f32)).astype(bf16)
        both = jnp.concatenate([kv, foreign], axis=0)
        totals = [
            total
            + mm(q, w_query, NT)
            + mm(terms[:, :width], w_key, NT)
            + mm(terms[:, width:], w_value, NT)
            for total, q, terms in (
                (totals[0], near[:own_rows], kv),
                (totals[1], near[own_rows:], foreign),
            )
        ]
        return totals, *summed([both, to_core(both)])

    near_0, far_0, own_0, flip_0, side_0, back_0, diag_0 = edges(0)
    q_0 = chip_terms(near_0, far_0)
    inner_0, back_0 = to_inner(diag_0), to_outer(back_0)
    side_0 = to_inner(after(side_0, q_0[0]))
    near_1, far_1, own_1, flip_1, side_1, back_1, diag_1 = edges(1, q_0[0], out_weight_grad)
    q_1 = chip_terms(near_1, far_1)
    flip_0 = after(flip_0, far_1)
    cross_0 = crossed(flip_0, inner_0)
    inner_1 = to_inner(after(diag_1, inner_0, q_0[1]))
    query_grad, q_sent = summed(q_0, q_1)
    side_0, back_0 = after((side_0, back_0), q_sent)
    cross_1 = crossed(after(flip_1, q_sent), inner_1)
    totals, kv_grad_0, kv_sent = finish(
        0, (0.0, 0.0), q_0[0], own_0, side_0, back_0, after(cross_0, q_sent, query_grad)
    )
    side_1, back_1 = after((side_1, back_1), inner_1, q_sent)
    side_1, back_1 = after((to_inner(side_1), to_outer(back_1)), kv_sent)
    totals, kv_grad_1, _ = finish(
        1, totals, q_1[0], own_1, side_1, back_1, after(cross_1, kv_sent)
    )
    grad_partner = to_partner(after(totals[1], kv_grad_0).astype(bf16))
    input_grad = totals[0] + grad_partner.astype(f32)
    key_grads = [grad[:, :width] for grad in (kv_grad_0, kv_grad_1)]
    value_grads = [grad[:, width:] for grad in (kv_grad_0, kv_grad_1)]

    def joined(pieces):
        return jnp.concatenate(pieces, axis=1)[None]

    return (
        input_grad.astype(bf16),
        query_grad[None],
        joined(key_grads),
        joined(value_grads),
        out_weight_grad[None],
    )


def solution(mesh):
    placed = (
        P(("blk", "rep"), None),
        P(("blk", "rep"), None),
        P(("blk", "rep"), None),
        P(),
        P(),
        P(),
        P(),
        P(("blk", "rep"), None, None),
        P(("blk", "rep"), None, None, None),
        P(("blk", "rep")),
    )
    return jax.shard_map(
        on_device,
        mesh=mesh,
        in_specs=placed,
        out_specs=(
            P(("blk", "rep"), None),
            P("blk", "rep", None),
            P("blk", "rep", None),
            P("blk", "rep", None),
            P("blk", "rep", None),
        ),
        check_vma=False,
    )
```
